128 devices in a mesh: gx: 16 (over x, y), gy: 8 (over z, core).
Axes of the slice: x: 4, y: 4, z: 4, core: 2. Of those that a mesh axis runs over, the one named last changes fastest.
Arguments:
- conserved: float32 [16384, 5, 512], P(('gx', 'gy')), may hold values from -4 to 17, as said below
- order_class: int32 [16384], P(('gx', 'gy')), may hold values from 0 to 4
- new_owner: int32 [16384], P(('gx', 'gy')), may hold values from 0 to 127, as said below
- neighbours: int32 [16384, 6], P(('gx', 'gy')), may hold values from 0 to 16383, as said below
Outputs:
- evolved: float32 [16384, 5, 512], P(('gx', 'gy'))
The draws below stay inside these ranges and needn't reach their ends.
Inputs may be any that keep to these rules, and one draw needn't show every extreme that they name: `conserved`: density between 0.2 and 2, pressure between 0.05 and 2, each velocity component between -2 and 2, with energy = pressure / 0.4 + kinetic energy. `new_owner`: an element keeps its slot: it goes from slot s of device d to slot s of device d XOR o_s, o_s depending on s only; at most 2 elements go from one device to any one device, and in every draw some pair of devices moves exactly 2. Values are device * 128 + slot in the new layout (device index gx * size of gy + gy). Relations are mirrored (the +x neighbour of e has e as its -x neighbour, likewise y and z). x neighbours lie on the same device or on the next or previous device along gx, wrapping; y neighbours likewise along gy; z neighbours on the same device. Each device has exactly 32 elements whose +x neighbour is on another device and as many for -x, and 16 for each y side.
All inputs are finite; a program needn't handle non-finite values.
Results may differ from the reference program's by a relative error of at most 0.0002.
Values sent between devices are 32-bit elements; how exact they have to be, the bound alone decides.
A program may use at most 128 MiB of HBM per device.

```python
import math
import jax
import jax.numpy as jnp
from jax import lax

NODES_1D = 8
NCLS = 5
FIELDS = 5
NQ = 512
BX = 4
BY = 8
BZ = 4
ELEM_DEV = 128
ELEMENTS = 16384
CAP = 2
N_GX = 16
N_GY = 8


heat_ratio = 1.4


def draw_conserved(key, part):
    key = jax.random.fold_in(key, 11)
    subkeys = jax.random.split(key, 3)
    grid_shape = (ELEMENTS, NQ)
    density = jnp.exp(jax.random.uniform(subkeys[0], grid_shape, jnp.float32, math.log(0.2), math.log(2.0)))
    velocity = jnp.clip(0.5 * jax.random.normal(subkeys[1], (3,) + grid_shape, jnp.float32), -2.0, 2.0)
    pressure = jnp.exp(jax.random.uniform(subkeys[2], grid_shape, jnp.float32, math.log(0.05), math.log(2.0)))
    momentum = density[None] * velocity
    energy = pressure / (heat_ratio - 1.0) + 0.5 * density * jnp.sum(velocity * velocity, axis=0)
    stacked = jnp.concatenate([density[None], momentum, energy[None]], axis=0)
    return jnp.transpose(stacked, (1, 0, 2)).astype(jnp.float32)


def draw_new_owner(key, part):
    key = jax.random.fold_in(key, 23)
    subkeys = jax.random.split(key, 3)
    devices = N_GX * N_GY
    multiset = jnp.arange(CAP * devices, dtype=jnp.int32) // CAP
    chosen_value = jax.random.randint(subkeys[0], (), 0, devices)
    scores = jax.random.permutation(subkeys[1], CAP * devices).astype(jnp.int32)
    scores = jnp.where(multiset == chosen_value, scores - CAP * devices, scores)
    ranking = jnp.argsort(scores, stable=True)
    offsets = jax.random.permutation(subkeys[2], multiset[ranking[:ELEM_DEV]])
    owners = jnp.bitwise_xor(jnp.arange(devices, dtype=jnp.int32)[:, None], offsets[None, :])
    return owners.reshape(-1).astype(jnp.int32)


def draw_neighbours(key, part):
    key = jax.random.fold_in(key, 37)
    devices = N_GX * N_GY
    cell_count = BX * BY * BZ
    slot_of_cell = jax.vmap(lambda device_id: jax.random.permutation(jax.random.fold_in(key, device_id), cell_count))(jnp.arange(devices)).astype(jnp.int32)
    cell_of_slot = jnp.argsort(slot_of_cell, axis=1, stable=True).astype(jnp.int32)
    cell_ids = jnp.arange(cell_count, dtype=jnp.int32)[None, :]
    cell_x = cell_ids // (BY * BZ)
    cell_y = cell_ids // BZ % BY
    cell_z = cell_ids % BZ
    device_ids = jnp.arange(devices, dtype=jnp.int32)[:, None]
    device_x = device_ids // N_GY
    device_y = device_ids % N_GY

    def global_row(dev_x, dev_y, pos_x, pos_y, pos_z):
        owner, pos_x, pos_y, pos_z = jnp.broadcast_arrays(dev_x * N_GY + dev_y, pos_x, pos_y, pos_z)
        cell = (pos_x * BY + pos_y) * BZ + pos_z
        return owner * cell_count + slot_of_cell[owner, cell]
    faces = []
    for step_by in (-1, 1):
        moved_x = cell_x + step_by
        crossing = (moved_x < 0) | (moved_x >= BX)
        faces.append(global_row(jnp.where(crossing, (device_x + step_by) % N_GX, device_x), device_y, moved_x % BX, cell_y, cell_z))
    for step_by in (-1, 1):
        moved_y = cell_y + step_by
        crossing = (moved_y < 0) | (moved_y >= BY)
        faces.append(global_row(device_x, jnp.where(crossing, (device_y + step_by) % N_GY, device_y), cell_x, moved_y % BY, cell_z))
    for step_by in (-1, 1):
        faces.append(global_row(device_x, device_y, cell_x, cell_y, (cell_z + step_by) % BZ))
    by_cell = jnp.stack(faces, axis=-1)
    by_slot = jnp.take_along_axis(by_cell, cell_of_slot[:, :, None], axis=1)
    return by_slot.reshape(devices * cell_count, 6).astype(jnp.int32)


def place_ends(array, rng, low, largest):
    dims = array.shape
    index_at = [jax.random.randint(jax.random.fold_in(rng, axis), (), 0, dims[axis]) for axis in range(len(dims))]
    array = array.at[tuple(index_at)].set(low)
    longest = dims.index(max(dims))
    index_at[longest] = (index_at[longest] + 1) % dims[longest]
    return array.at[tuple(index_at)].set(largest)


def setup_inputs(seed: int = 0) -> dict:
    streams_of = jax.random.split(jax.random.key(seed), 5)
    conserved = draw_conserved(jax.random.fold_in(streams_of[4], 71), 0)
    order_class = place_ends(jax.random.randint(streams_of[1], (ELEMENTS,), 0, NCLS), jax.random.fold_in(streams_of[1], 1), 0, NCLS - 1).astype(jnp.int32)
    new_owner = draw_new_owner(jax.random.fold_in(streams_of[4], 71), 0)
    neighbours = draw_neighbours(jax.random.fold_in(streams_of[4], 71), 0)
    return {"conserved": conserved, "order_class": order_class, "new_owner": new_owner, "neighbours": neighbours}


heat_ratio = 1.4
rho_floor = 0.25
press_floor = 0.1
time_step = 0.005
full_precision = lax.Precision.HIGHEST

def legendre_row(position, points):
    table = [1.0, position]
    for order in range(1, points - 1):
        table.append(((2 * order + 1) * position * table[order] - order * table[order - 1]) / (order + 1))
    return table[:points]

def node_tables(points, classes):
    degree = points - 1
    abscissae = [-math.cos(math.pi * index / degree) for index in range(points)]
    for newton_step in range(100):
        for index in range(1, degree):
            spot = abscissae[index]
            table = legendre_row(spot, points)
            abscissae[index] = spot - (spot * table[degree] - table[degree - 1]) / (points * table[degree])
    vander = [legendre_row(spot, points) for spot in abscissae]
    values = [table[degree] for table in vander]
    weights = [2.0 / (degree * (degree + 1) * value * value) for value in values]
    derivative = []
    for row_index in range(points):
        entries = []
        for col_index in range(points):
            if row_index == col_index:
                entries.append(0.0)
            else:
                entries.append(values[row_index] / (values[col_index] * (abscissae[row_index] - abscissae[col_index])))
        derivative.append(entries)
    derivative[0][0] = -degree * (degree + 1) / 4.0
    derivative[degree][degree] = degree * (degree + 1) / 4.0
    norms = [sum((weights[index] * vander[index][mode] ** 2 for index in range(points))) for mode in range(points)]
    filters = []
    for k in range(classes):
        flat = []
        for row_index in range(points):
            for col_index in range(points):
                flat.append(sum((vander[row_index][mode] * vander[col_index][mode] * weights[col_index] / norms[mode] for mode in range(degree - k + 1))))
        filters.append(flat)
    return (jnp.asarray(derivative, jnp.float32), jnp.asarray(filters, jnp.float32), float(1.0 / weights[0]))

def primitive(values):
    density = jnp.maximum(values[..., 0, :], rho_floor)
    momentum = values[..., 1:4, :]
    velocity = momentum / density[..., None, :]
    kinetic = 0.5 * lax.optimization_barrier(jnp.sum(momentum * velocity, axis=-2))
    pressure = jnp.maximum((heat_ratio - 1.0) * (values[..., 4, :] - kinetic), press_floor)
    return (density, velocity, pressure)

def flux_along(values, direction):
    density, velocity, pressure = primitive(values)
    normal = velocity[..., direction, :]
    entries = [values[..., 1 + direction, :]]
    for component in range(3):
        momentum_row = values[..., 1 + component, :] * normal
        if component == direction:
            momentum_row = momentum_row + pressure
        entries.append(momentum_row)
    entries.append((values[..., 4, :] + pressure) * normal)
    signal = jnp.abs(normal) + jnp.sqrt(heat_ratio * pressure / density)
    return (jnp.stack(entries, axis=-2), signal)

def rusanov(left_state, left_flux, left_signal, right_state, right_flux, right_signal):
    fastest = jnp.maximum(left_signal, right_signal)
    return 0.5 * (left_flux + right_flux) - 0.5 * fastest[..., None, :] * (right_state - left_state)

def derive(derivative, node_cube, direction):
    patterns = ['ij,efjbc->efibc', 'ij,efajc->efaic', 'ij,efabj->efabi']
    return jnp.einsum(patterns[direction], derivative, node_cube, precision=full_precision)

def project(element_filters, node_cube):
    node_cube = jnp.einsum('eij,efjbc->efibc', element_filters, node_cube, precision=full_precision)
    node_cube = jnp.einsum('eij,efajc->efaic', element_filters, node_cube, precision=full_precision)
    return jnp.einsum('eij,efabj->efabi', element_filters, node_cube, precision=full_precision)

def face_of(node_cube, direction, which):
    sliced = lax.index_in_dim(node_cube, which, 2 + direction, keepdims=False)
    return sliced.reshape(node_cube.shape[0], node_cube.shape[1], -1)

def add_face(tendency, direction, which, contribution):
    points = tendency.shape[-1]
    contribution = contribution.reshape(tendency.shape[0], tendency.shape[1], points, points)
    selector = (slice(None),) * (2 + direction) + (which,)
    return tendency.at[selector].add(contribution)

def evaluate(values, element_filters, derivative, lifting, neighbours):
    points = NODES_1D
    node_cube = values.reshape(values.shape[0], FIELDS, points, points, points)
    tendency = jnp.zeros_like(node_cube)
    for direction in range(3):
        fluxes, _ = flux_along(values, direction)
        tendency = tendency - derive(derivative, fluxes.reshape(node_cube.shape), direction)
    for direction in range(3):
        low_trace = face_of(node_cube, direction, 0)
        high_trace = face_of(node_cube, direction, points - 1)
        low_flux, low_signal = flux_along(low_trace, direction)
        high_flux, high_signal = flux_along(high_trace, direction)
        next_ids = neighbours[:, 2 * direction + 1]
        before = neighbours[:, 2 * direction]
        numerical = rusanov(high_trace, high_flux, high_signal, low_trace[next_ids], low_flux[next_ids], low_signal[next_ids])
        tendency = add_face(tendency, direction, points - 1, -lifting * (numerical - high_flux))
        numerical = rusanov(high_trace[before], high_flux[before], high_signal[before], low_trace, low_flux, low_signal)
        tendency = add_face(tendency, direction, 0, lifting * (numerical - low_flux))
    return project(element_filters, tendency).reshape(values.shape)

def reference(conserved, order_class, new_owner, neighbours):
    row_ids = jnp.arange(conserved.shape[0], dtype=jnp.int32)
    target = (new_owner * ELEM_DEV + row_ids % ELEM_DEV).astype(jnp.int32)
    migrated = jnp.zeros_like(conserved).at[target].set(conserved)
    classes = jnp.zeros_like(order_class).at[target].set(order_class)
    derivative, filters, lifting = node_tables(NODES_1D, NCLS)
    chosen = (classes[:, None] == jnp.arange(NCLS, dtype=jnp.int32)[None, :]).astype(jnp.float32)
    element_filters = jnp.dot(chosen, filters, precision=full_precision).reshape(-1, NODES_1D, NODES_1D)
    cube_shape = (conserved.shape[0], FIELDS, NODES_1D, NODES_1D, NODES_1D)
    initial = project(element_filters, migrated.reshape(cube_shape)).reshape(conserved.shape)
    section_one = initial + time_step * evaluate(initial, element_filters, derivative, lifting, neighbours)
    return 0.5 * initial + 0.5 * (section_one + time_step * evaluate(section_one, element_filters, derivative, lifting, neighbours))
```

```python
import math

import jax
import jax.numpy as jnp
import numpy as np
from jax import lax
from jax.experimental import pallas as pl
from jax.experimental.pallas import tpu as pltpu
from jax.sharding import PartitionSpec as P

NODES = 8
NCLS = 5
FIELDS = 5
NQ = 512
ELEM = 128
LANES = 128
STRIDE = 48
ROWS = 41
heat_ratio = 1.4
rho_floor = 0.25
press_floor = 0.1
time_step = 0.005
MESH = pl.DeviceIdType.MESH
f32 = jnp.float32
bf16 = jnp.bfloat16


def legendre_row(position, points):
    table = [1.0, position]
    for order in range(1, points - 1):
        table.append(
            ((2 * order + 1) * position * table[order] - order * table[order - 1]) / (order + 1)
        )
    return table[:points]


def node_tables(points, classes):
    degree = points - 1
    abscissae = [-math.cos(math.pi * index / degree) for index in range(points)]
    for newton_step in range(100):
        for index in range(1, degree):
            spot = abscissae[index]
            table = legendre_row(spot, points)
            abscissae[index] = spot - (spot * table[degree] - table[degree - 1]) / (
                points * table[degree]
            )
    vander = [legendre_row(spot, points) for spot in abscissae]
    values = [table[degree] for table in vander]
    weights = [2.0 / (degree * (degree + 1) * value * value) for value in values]
    derivative = np.zeros((points, points))
    for i in range(points):
        for j in range(points):
            if i != j:
                derivative[i, j] = values[i] / (values[j] * (abscissae[i] - abscissae[j]))
    derivative[0, 0] = -degree * (degree + 1) / 4.0
    derivative[degree, degree] = degree * (degree + 1) / 4.0
    vand = np.array(vander)
    wts = np.array(weights)
    norms = (wts[:, None] * vand**2).sum(axis=0)
    filters = np.zeros((classes, points, points))
    for k in range(classes):
        kept = degree - k + 1
        filters[k] = (vand[:, :kept] / norms[:kept]) @ (vand[:, :kept].T * wts)
    return derivative, filters, float(1.0 / weights[0])


DERIV, FILTERS, LIFT = node_tables(NODES, NCLS)
DER_ODD = 0.5 * (DERIV[:4, :4] - DERIV[:4, :3:-1])
DER_EVEN = 0.5 * (DERIV[:4, :4] + DERIV[:4, :3:-1])
FIL_EVEN = 0.5 * (FILTERS[:, :4, :4] + FILTERS[:, :4, :3:-1])
FIL_ODD = 0.5 * (FILTERS[:, :4, :4] - FILTERS[:, :4, :3:-1])


def rotation_tables():
    rows = np.arange(NODES)
    out = np.zeros((NODES * (NCLS + 1), NODES, LANES), np.float32)
    for r in range(NODES):
        for k in range(NCLS):
            out[k * NODES + r] = FILTERS[k][rows, (rows + r) % NODES][:, None]
        out[NCLS * NODES + r] = DERIV[rows, (rows + r) % NODES][:, None]
    return out


def split_two(value):
    high = value.astype(bf16)
    low = (value - high.astype(f32)).astype(bf16)
    return high, low


def iota2(shape, dim):
    return lax.broadcasted_iota(jnp.int32, shape, dim)


def migrate_kernel(x_ref, owner_ref, class_ref, u_ref, cls_ref, stage, landed, send_sem, recv_sem, own_sem):
    gx = lax.axis_index("gx")
    gy = lax.axis_index("gy")
    ngy = lax.axis_size("gy")
    devices = ELEM
    me = gx * ngy + gy
    barrier = pltpu.get_barrier_semaphore()

    def greet(r, carry):
        t = lax.rem(me + r, devices)
        pl.semaphore_signal(barrier, inc=1, device_id=(t // ngy, lax.rem(t, ngy)), device_id_type=MESH)
        return carry

    lax.fori_loop(1, devices, greet, 0)

    owner = jnp.broadcast_to(owner_ref[...], (ELEM, ELEM))
    owner_f = owner.astype(f32)
    same = owner_f == owner_f.T
    earlier = iota2((ELEM, ELEM), 0) < iota2((ELEM, ELEM), 1)
    rank = jnp.sum(jnp.where(same & earlier, 1.0, 0.0), axis=0, keepdims=True)
    hit = iota2((ELEM, ELEM), 0) == owner
    first = jnp.where(hit & (rank < 0.5), 1.0, 0.0)
    second = jnp.where(hit & (rank > 0.5), 1.0, 0.0)
    pick = jnp.concatenate([first, second], axis=0).astype(bf16)
    pick_twice = jnp.concatenate([pick, pick], axis=1)
    for f in range(FIELDS):
        high, low = split_two(x_ref[f])
        rows = jnp.dot(pick_twice, jnp.concatenate([high, low], axis=0), preferred_element_type=f32)
        for c in range(2):
            for q in range(4):
                stage[pl.ds(c * 20 + f * 4 + q, ELEM, stride=STRIDE), :] = rows[
                    c * ELEM : (c + 1) * ELEM, q * LANES : (q + 1) * LANES
                ]
    stage[pl.ds(40, ELEM, stride=STRIDE), :] = jnp.broadcast_to(class_ref[...].astype(f32), (ELEM, ELEM))

    pl.semaphore_wait(barrier, devices - 1)

    def here(t):
        return pl.ds(pl.multiple_of(t * STRIDE, 8), ROWS)

    def send(r, carry):
        t = lax.rem(me + lax.rem(r * 37, devices), devices)
        pltpu.make_async_remote_copy(
            src_ref=stage.at[here(t)],
            dst_ref=landed.at[here(me)],
            send_sem=send_sem.at[t],
            recv_sem=recv_sem.at[me],
            device_id=(t // ngy, lax.rem(t, ngy)),
            device_id_type=MESH,
        ).start()
        return carry

    own = pltpu.make_async_copy(stage.at[here(me)], landed.at[here(me)], own_sem)
    own.start()
    lax.fori_loop(1, devices, send, 0)
    own.wait()

    def arrive(r, carry):
        t = lax.rem(me + devices - lax.rem(r * 37, devices), devices)
        pltpu.make_async_remote_copy(
            src_ref=stage.at[here(t)],
            dst_ref=landed.at[here(t)],
            send_sem=send_sem.at[t],
            recv_sem=recv_sem.at[t],
            device_id=(t // ngy, lax.rem(t, ngy)),
            device_id_type=MESH,
        ).wait_recv()
        return carry

    lax.fori_loop(1, devices, arrive, 0)

    place = jnp.concatenate([first.T, second.T], axis=1).astype(bf16)
    place = jnp.concatenate([place, place], axis=1)
    for f in range(FIELDS):
        for q in range(4):
            r = f * 4 + q
            both = jnp.concatenate(
                [landed[pl.ds(r, ELEM, stride=STRIDE), :], landed[pl.ds(20 + r, ELEM, stride=STRIDE), :]], axis=0
            )
            high, low = split_two(both)
            block = jnp.dot(place, jnp.concatenate([high, low], axis=0), preferred_element_type=f32)
            u_ref[f, pl.ds(q * LANES, LANES), :] = block.T
    classes = landed[pl.ds(40, ELEM, stride=STRIDE), :]
    cls_ref[...] = jnp.sum(jnp.where(hit, classes, 0.0), axis=0, keepdims=True)

    def sent(r, carry):
        t = lax.rem(me + r, devices)
        pltpu.make_async_remote_copy(
            src_ref=stage.at[here(t)],
            dst_ref=landed.at[here(t)],
            send_sem=send_sem.at[t],
            recv_sem=recv_sem.at[t],
            device_id=(t // ngy, lax.rem(t, ngy)),
            device_id_type=MESH,
        ).wait_send()
        return carry

    lax.fori_loop(1, devices, sent, 0)


def migrate(conserved, order_class, new_owner):
    return pl.pallas_call(
        migrate_kernel,
        out_shape=(
            jax.ShapeDtypeStruct((FIELDS, NQ, ELEM), f32),
            jax.ShapeDtypeStruct((1, ELEM), f32),
        ),
        in_specs=[pl.BlockSpec(memory_space=pltpu.VMEM)] * 3,
        out_specs=(pl.BlockSpec(memory_space=pltpu.VMEM),) * 2,
        scratch_shapes=[
            pltpu.VMEM((ELEM * STRIDE, LANES), f32),
            pltpu.VMEM((ELEM * STRIDE, LANES), f32),
            pltpu.SemaphoreType.DMA((ELEM,)),
            pltpu.SemaphoreType.DMA((ELEM,)),
            pltpu.SemaphoreType.DMA,
        ],
        compiler_params=pltpu.CompilerParams(collective_id=0, has_side_effects=True, vmem_limit_bytes=40 << 20),
        name="migrate",
    )(conserved, new_owner.reshape(1, ELEM), order_class.reshape(1, ELEM))


def mirrored(lines, even, odd):
    sums = [lines[m] + lines[7 - m] for m in range(4)]
    diffs = [lines[m] - lines[7 - m] for m in range(4)]
    top, bottom = [], []
    for k in range(4):
        a = even(k, 0) * sums[0]
        b = odd(k, 0) * diffs[0]
        for m in range(1, 4):
            a = a + even(k, m) * sums[m]
            b = b + odd(k, m) * diffs[m]
        top.append(a + b)
        bottom.append((a, b))
    return top, bottom


def filter_lines(lines, coef):
    top, parts = mirrored(lines, lambda k, m: coef[k * 4 + m], lambda k, m: coef[16 + k * 4 + m])
    return top + [parts[k][0] - parts[k][1] for k in (3, 2, 1, 0)]


def derive_lines(lines):
    top, parts = mirrored(lines, lambda k, m: float(DER_EVEN[k, m]), lambda k, m: float(DER_ODD[k, m]))
    return top + [parts[k][1] - parts[k][0] for k in (3, 2, 1, 0)]


def rotated(tile, coef):
    total = coef[0] * tile
    for r in range(1, NODES):
        total = total + coef[r] * pltpu.roll(tile, NODES - r, 0)
    return total


def primitive(u):
    inverse = 1.0 / jnp.maximum(u[0], rho_floor)
    vel = [u[1] * inverse, u[2] * inverse, u[3] * inverse]
    kinetic = 0.5 * (u[1] * vel[0] + u[2] * vel[1] + u[3] * vel[2])
    pressure = jnp.maximum((heat_ratio - 1.0) * (u[4] - kinetic), press_floor)
    return inverse, vel, pressure


def flux_of(u, prim, a):
    _, vel, pressure = prim
    v = vel[a]
    out = [u[1 + a]]
    for c in range(3):
        m = u[1 + c] * v
        out.append(m + pressure if c == a else m)
    out.append((u[4] + pressure) * v)
    return out


def signal_of(prim, a):
    inverse, vel, pressure = prim
    return jnp.abs(vel[a]) + jnp.sqrt(heat_ratio * pressure * inverse)


def take(tile, index):
    return jnp.take_along_axis(tile, index, axis=1)


def sections_kernel(
    u_in, cls_ref, nb_ref, tab_ref, out_ref,
    u0, u1, tend, fil, rot, ids, packx, packy, gotx, goty, sx, rx, sy, ry,
):
    gx = lax.axis_index("gx")
    gy = lax.axis_index("gy")
    ngx = lax.axis_size("gx")
    ngy = lax.axis_size("gy")
    me = gx * ngy + gy
    peers = [
        (lax.rem(gx + ngx - 1, ngx), gy),
        (lax.rem(gx + 1, ngx), gy),
        (gx, lax.rem(gy + ngy - 1, ngy)),
        (gx, lax.rem(gy + 1, ngy)),
    ]
    barrier = pltpu.get_barrier_semaphore()
    for peer in peers:
        pl.semaphore_signal(barrier, inc=1, device_id=peer, device_id_type=MESH)

    cls = jnp.broadcast_to(cls_ref[...], (NODES, LANES))
    is_class = [jnp.where(cls == float(k), 1.0, 0.0) for k in range(NCLS)]
    for n in range(16):
        e = is_class[0] * float(FIL_EVEN[0, n // 4, n % 4])
        o = is_class[0] * float(FIL_ODD[0, n // 4, n % 4])
        for k in range(1, NCLS):
            e = e + is_class[k] * float(FIL_EVEN[k, n // 4, n % 4])
            o = o + is_class[k] * float(FIL_ODD[k, n // 4, n % 4])
        fil[n] = e
        fil[16 + n] = o
    for r in range(NODES):
        e = is_class[0] * tab_ref[r]
        for k in range(1, NCLS):
            e = e + is_class[k] * tab_ref[k * NODES + r]
        rot[r] = e

    nb = nb_ref[...]
    slot = lax.rem(nb, ELEM)
    away = jnp.where(nb // ELEM != me, 1.0, 0.0)
    stacked = jnp.concatenate([away, slot.astype(f32), jnp.zeros((116, LANES), f32)], axis=0).T
    lower = iota2((ELEM, ELEM), 0) < iota2((ELEM, ELEM), 1)
    lane = iota2((ELEM, ELEM), 1)
    row_f = iota2((ELEM, ELEM), 0).astype(f32)
    awaits = []
    for face in range(4):
        rim = 32 if face < 2 else 16
        away_col = stacked[:, face : face + 1]
        slot_col = stacked[:, 6 + face : 7 + face]
        away_row = away[face : face + 1]
        slot_row = slot[face : face + 1].astype(f32)
        upto = jnp.where(iota2((ELEM, ELEM), 1) < iota2((ELEM, ELEM), 0), jnp.broadcast_to(away_row, (ELEM, ELEM)), 0.0)
        rank_col = jnp.sum(upto, axis=1, keepdims=True)
        chosen = (away_col > 0.5) & (rank_col == lax.rem(lane, rim).astype(f32))
        order = jnp.sum(jnp.where(chosen, row_f, 0.0), axis=0, keepdims=True)
        ids[face] = jnp.broadcast_to(order.astype(jnp.int32), (NODES, LANES))
        mark = (away_col > 0.5) & (slot_col < slot_row)
        arrival = jnp.sum(jnp.where(mark, 1.0, 0.0), axis=0, keepdims=True)
        ids[4 + face] = jnp.broadcast_to(arrival.astype(jnp.int32), (NODES, LANES))
        ids[8 + face] = jnp.broadcast_to((away_row > 0.5).astype(jnp.int32), (NODES, LANES))
    for face in range(6):
        ids[12 + face] = jnp.broadcast_to(slot[face : face + 1], (NODES, LANES))

    def project(src, finish):
        coef = [fil[n] for n in range(32)]

        def along_i(n, carry):
            f = n // NODES
            j = lax.rem(n, NODES)
            lines = filter_lines([src[f, i, j] for i in range(NODES)], coef)
            for i in range(NODES):
                src[f, i, j] = lines[i]
            return carry

        lax.fori_loop(0, FIELDS * NODES, along_i, 0)
        turn = [rot[r] for r in range(NODES)]

        def along_jl(n, carry):
            f = n // NODES
            i = lax.rem(n, NODES)
            lines = filter_lines([src[f, i, j] for j in range(NODES)], coef)
            for j in range(NODES):
                finish(f, i, j, rotated(lines[j], turn))
            return carry

        lax.fori_loop(0, FIELDS * NODES, along_jl, 0)

    def load_in(n, carry):
        f = n // NODES
        i = lax.rem(n, NODES)
        for j in range(NODES):
            u0[f, i, j] = u_in[f, pl.ds(pl.multiple_of(i * 64 + j * 8, 8), 8), :]
        return carry

    lax.fori_loop(0, FIELDS * NODES, load_in, 0)

    def put_initial(f, i, j, value):
        u0[f, i, j] = value

    project(u0, put_initial)

    pl.semaphore_wait(barrier, 4)

    def copies(step):
        out = []
        for face in range(4):
            back = face + 1 - 2 * (face % 2)
            pack, got, ss, rs = (packx, gotx, sx, rx) if face < 2 else (packy, goty, sy, ry)
            side = face % 2
            other = back % 2
            out.append(
                pltpu.make_async_remote_copy(
                    src_ref=pack.at[step, side],
                    dst_ref=got.at[step, other],
                    send_sem=ss.at[step, side],
                    recv_sem=rs.at[step, other],
                    device_id=peers[face],
                    device_id_type=MESH,
                )
            )
        return out

    lane8 = iota2((NODES, LANES), 1)

    def face_tile(src, a, end, f, k):
        if a == 0:
            return src[f, 7 * end, k]
        return src[f, k, 7 * end]

    def pack_faces(src, step):
        for face in range(4):
            a, end = face // 2, face % 2
            order = ids[face]
            rim = 32 if face < 2 else 16
            groups = LANES // rim
            width = 40 // groups
            pack = packx if face < 2 else packy
            for m in range(width):
                total = None
                for g in range(groups):
                    t = g * width + m
                    piece = take(face_tile(src, a, end, t // NODES, t % NODES), order)
                    total = piece if total is None else jnp.where(lane8 >= g * rim, piece, total)
                pack[step, end, pl.ds(m * 8, 8), :] = total

    def section(src, step, finish):
        pack_faces(src, step)
        moving = copies(step)
        for c in moving:
            c.start()

        def along_x(j, carry):
            fluxes = []
            for i in range(NODES):
                u = [src[f, i, j] for f in range(FIELDS)]
                fluxes.append(flux_of(u, primitive(u), 0))
            for f in range(FIELDS):
                lines = derive_lines([fluxes[i][f] for i in range(NODES)])
                for i in range(NODES):
                    tend[f, i, j] = -lines[i]
            return carry

        lax.fori_loop(0, NODES, along_x, 0)
        turn = [tab_ref[NCLS * NODES + r] for r in range(NODES)]

        def along_yz(i, carry):
            fluxes = []
            for j in range(NODES):
                u = [src[f, i, j] for f in range(FIELDS)]
                prim = primitive(u)
                fluxes.append(flux_of(u, prim, 1))
                along = flux_of(u, prim, 2)
                for f in range(FIELDS):
                    tend[f, i, j] = tend[f, i, j] - rotated(along[f], turn)
            for f in range(FIELDS):
                lines = derive_lines([fluxes[j][f] for j in range(NODES)])
                for j in range(NODES):
                    tend[f, i, j] = tend[f, i, j] - lines[j]
            return carry

        lax.fori_loop(0, NODES, along_yz, 0)

        def jump(inner, outer, a, end):
            p_in = primitive(inner)
            p_out = primitive(outer)
            f_in = flux_of(inner, p_in, a)
            f_out = flux_of(outer, p_out, a)
            fastest = jnp.maximum(signal_of(p_in, a), signal_of(p_out, a))
            out = []
            for f in range(FIELDS):
                change = 0.5 * (f_out[f] - f_in[f])
                if end == 1:
                    out.append(-LIFT * (change - 0.5 * fastest * (outer[f] - inner[f])))
                else:
                    out.append(LIFT * (change - 0.5 * fastest * (inner[f] - outer[f])))
            return out

        z_slots = (ids[16], ids[17])

        def z_faces(i, carry):
            low = [src.at[f, i].reshape(64, LANES)[pl.ds(0, 8, stride=8), :] for f in range(FIELDS)]
            high = [src.at[f, i].reshape(64, LANES)[pl.ds(7, 8, stride=8), :] for f in range(FIELDS)]
            w = [take(low[f], z_slots[1]) for f in range(FIELDS)]
            add = jump(high, w, 2, 1)
            for f in range(FIELDS):
                t = tend.at[f, i].reshape(64, LANES)
                t[pl.ds(7, 8, stride=8), :] = t[pl.ds(7, 8, stride=8), :] + add[f]
            w = [take(high[f], z_slots[0]) for f in range(FIELDS)]
            add = jump(low, w, 2, 0)
            for f in range(FIELDS):
                t = tend.at[f, i].reshape(64, LANES)
                t[pl.ds(0, 8, stride=8), :] = t[pl.ds(0, 8, stride=8), :] + add[f]
            return carry

        lax.fori_loop(0, NODES, z_faces, 0)

        for face in range(4):
            moving[face].wait_recv()

        for face in range(4):
            a, end = face // 2, face % 2
            rim = 32 if face < 2 else 16
            groups = LANES // rim
            width = 40 // groups
            got = gotx if face < 2 else goty
            local = ids[12 + face]
            arrival = ids[4 + face]
            remote = ids[8 + face] > 0
            for k in range(NODES):
                inner = [face_tile(src, a, end, f, k) for f in range(FIELDS)]
                outer = []
                for f in range(FIELDS):
                    t = f * NODES + k
                    near = take(face_tile(src, a, 1 - end, f, k), local)
                    far = take(got[step, end, pl.ds((t % width) * 8, 8), :], arrival + (t // width) * rim)
                    outer.append(jnp.where(remote, far, near))
                add = jump(inner, outer, a, end)
                for f in range(FIELDS):
                    if a == 0:
                        tend[f, 7 * end, k] = tend[f, 7 * end, k] + add[f]
                    else:
                        tend[f, k, 7 * end] = tend[f, k, 7 * end] + add[f]

        project(tend, finish)
        return moving

    def put_first(f, i, j, value):
        u1[f, i, j] = u0[f, i, j] + time_step * value

    started = section(u0, 0, put_first)

    def put_last(f, i, j, value):
        u0[f, i, j] = 0.5 * u0[f, i, j] + 0.5 * (u1[f, i, j] + time_step * value)

    started = started + section(u1, 1, put_last)

    def turn_back(n, carry):
        f = n // 4
        q = lax.rem(n, 4)
        block = u0[f, pl.ds(q * 2, 2)].reshape(LANES, LANES)
        out_ref[f, :, pl.ds(pl.multiple_of(q * LANES, LANES), LANES)] = block.T
        return carry

    lax.fori_loop(0, FIELDS * 4, turn_back, 0)
    for c in started:
        c.wait_send()


def sections(state, classes, neighbours):
    cube = (FIELDS, NODES, NODES, NODES, LANES)
    return pl.pallas_call(
        sections_kernel,
        out_shape=jax.ShapeDtypeStruct((FIELDS, ELEM, NQ), f32),
        in_specs=[pl.BlockSpec(memory_space=pltpu.VMEM)] * 4,
        out_specs=pl.BlockSpec(memory_space=pltpu.VMEM),
        scratch_shapes=[
            pltpu.VMEM(cube, f32),
            pltpu.VMEM(cube, f32),
            pltpu.VMEM(cube, f32),
            pltpu.VMEM((32, NODES, LANES), f32),
            pltpu.VMEM((NODES, NODES, LANES), f32),
            pltpu.VMEM((18, NODES, LANES), jnp.int32),
            pltpu.VMEM((2, 2, 80, LANES), f32),
            pltpu.VMEM((2, 2, 40, LANES), f32),
            pltpu.VMEM((2, 2, 80, LANES), f32),
            pltpu.VMEM((2, 2, 40, LANES), f32),
            pltpu.SemaphoreType.DMA((2, 2)),
            pltpu.SemaphoreType.DMA((2, 2)),
            pltpu.SemaphoreType.DMA((2, 2)),
            pltpu.SemaphoreType.DMA((2, 2)),
        ],
        compiler_params=pltpu.CompilerParams(collective_id=1, has_side_effects=True, vmem_limit_bytes=40 << 20),
        name="sections",
    )(state, classes, neighbours, jnp.asarray(rotation_tables()))


def shards(conserved, order_class, new_owner, neighbours):
    state, classes = migrate(jnp.transpose(conserved, (1, 0, 2)), order_class, new_owner)
    evolved = sections(state, classes, jnp.transpose(neighbours, (1, 0)))
    return jnp.transpose(evolved, (1, 0, 2))


def solution(mesh):
    in_specs = (
        P(("gx", "gy"), None, None),
        P(("gx", "gy")),
        P(("gx", "gy")),
        P(("gx", "gy"), None),
    )
    out_specs = P(("gx", "gy"), None, None)
    return jax.shard_map(shards, mesh=mesh, in_specs=in_specs, out_specs=out_specs, check_vma=False)
```

```python
import math

import jax
import jax.numpy as jnp
import numpy as np
from jax import lax
from jax.experimental import pallas as pl
from jax.experimental.pallas import tpu as pltpu
from jax.sharding import PartitionSpec as P

NODES = 8
NCLS = 5
FIELDS = 5
NQ = 512
ELEM = 128
LANES = 128
STRIDE = 48
ROWS = 41
CUBE = (FIELDS, NODES, NODES, NODES, LANES)
heat_ratio = 1.4
rho_floor = 0.25
press_floor = 0.1
time_step = 0.005
MESH = pl.DeviceIdType.MESH
RIMS = (32, 32, 16, 16)
UNROLL = 1
f32 = jnp.float32
bf16 = jnp.bfloat16


def legendre_row(position, points):
    table = [1.0, position]
    for order in range(1, points - 1):
        table.append(
            ((2 * order + 1) * position * table[order] - order * table[order - 1]) / (order + 1)
        )
    return table[:points]


def node_tables(points, classes):
    degree = points - 1
    abscissae = [-math.cos(math.pi * index / degree) for index in range(points)]
    for newton_step in range(100):
        for index in range(1, degree):
            spot = abscissae[index]
            table = legendre_row(spot, points)
            abscissae[index] = spot - (spot * table[degree] - table[degree - 1]) / (
                points * table[degree]
            )
    vander = [legendre_row(spot, points) for spot in abscissae]
    values = [table[degree] for table in vander]
    weights = [2.0 / (degree * (degree + 1) * value * value) for value in values]
    derivative = np.zeros((points, points))
    for i in range(points):
        for j in range(points):
            if i != j:
                derivative[i, j] = values[i] / (values[j] * (abscissae[i] - abscissae[j]))
    derivative[0, 0] = -degree * (degree + 1) / 4.0
    derivative[degree, degree] = degree * (degree + 1) / 4.0
    vand = np.array(vander)
    wts = np.array(weights)
    norms = (wts[:, None] * vand**2).sum(axis=0)
    filters = np.zeros((classes, points, points))
    for k in range(classes):
        kept = degree - k + 1
        filters[k] = (vand[:, :kept] / norms[:kept]) @ (vand[:, :kept].T * wts)
    return derivative, filters, float(1.0 / weights[0])


DERIV, FILTERS, LIFT = node_tables(NODES, NCLS)
DER_ODD = 0.5 * (DERIV[:4, :4] - DERIV[:4, :3:-1])
DER_EVEN = 0.5 * (DERIV[:4, :4] + DERIV[:4, :3:-1])
FIL_EVEN = 0.5 * (FILTERS[:, :4, :4] + FILTERS[:, :4, :3:-1])
FIL_ODD = 0.5 * (FILTERS[:, :4, :4] - FILTERS[:, :4, :3:-1])


def rotation_tables():
    rows = np.arange(NODES)
    out = np.zeros((NODES * (NCLS + 1), NODES, LANES), np.float32)
    for r in range(NODES):
        for k in range(NCLS):
            out[k * NODES + r] = FILTERS[k][rows, (rows + r) % NODES][:, None]
        out[NCLS * NODES + r] = DERIV[rows, (rows + r) % NODES][:, None]
    return out


def split_two(value):
    high = value.astype(bf16)
    low = (value - high.astype(f32)).astype(bf16)
    return high, low


def iota2(shape, dim):
    return lax.broadcasted_iota(jnp.int32, shape, dim)


def mirrored(lines, even, odd):
    sums = [lines[m] + lines[7 - m] for m in range(4)]
    diffs = [lines[m] - lines[7 - m] for m in range(4)]
    top, bottom = [], []
    for k in range(4):
        a = even(k, 0) * sums[0]
        b = odd(k, 0) * diffs[0]
        for m in range(1, 4):
            a = a + even(k, m) * sums[m]
            b = b + odd(k, m) * diffs[m]
        top.append(a + b)
        bottom.append((a, b))
    return top, bottom


def filter_lines(lines, coef):
    top, parts = mirrored(lines, lambda k, m: coef[k * 4 + m], lambda k, m: coef[16 + k * 4 + m])
    return top + [parts[k][0] - parts[k][1] for k in (3, 2, 1, 0)]


def derive_lines(lines):
    top, parts = mirrored(lines, lambda k, m: float(DER_EVEN[k, m]), lambda k, m: float(DER_ODD[k, m]))
    return top + [parts[k][1] - parts[k][0] for k in (3, 2, 1, 0)]


def rotated(tile, coef):
    total = coef[0] * tile
    for r in range(1, NODES):
        total = total + coef[r] * pltpu.roll(tile, NODES - r, 0)
    return total


def primitive(u):
    inverse = 1.0 / jnp.maximum(u[0], rho_floor)
    vel = [u[1] * inverse, u[2] * inverse, u[3] * inverse]
    kinetic = 0.5 * (u[1] * vel[0] + u[2] * vel[1] + u[3] * vel[2])
    pressure = jnp.maximum((heat_ratio - 1.0) * (u[4] - kinetic), press_floor)
    return inverse, vel, pressure


def flux_of(u, prim, a):
    _, vel, pressure = prim
    v = vel[a]
    out = [u[1 + a]]
    for c in range(3):
        m = u[1 + c] * v
        out.append(m + pressure if c == a else m)
    out.append((u[4] + pressure) * v)
    return out


def signal_of(prim, a):
    inverse, vel, pressure = prim
    return jnp.abs(vel[a]) + jnp.sqrt(heat_ratio * pressure * inverse)


def take(tile, index):
    return jnp.take_along_axis(tile, index, axis=1)


def class_tables(cls, tab_ref, fil, rot):
    cls = jnp.broadcast_to(cls, (NODES, LANES))
    is_class = [jnp.where(cls == float(k), 1.0, 0.0) for k in range(NCLS)]
    for n in range(16):
        e = is_class[0] * float(FIL_EVEN[0, n // 4, n % 4])
        o = is_class[0] * float(FIL_ODD[0, n // 4, n % 4])
        for k in range(1, NCLS):
            e = e + is_class[k] * float(FIL_EVEN[k, n // 4, n % 4])
            o = o + is_class[k] * float(FIL_ODD[k, n // 4, n % 4])
        fil[n] = e
        fil[16 + n] = o
    for r in range(NODES):
        e = is_class[0] * tab_ref[r]
        for k in range(1, NCLS):
            e = e + is_class[k] * tab_ref[k * NODES + r]
        rot[r] = e


def rim_tables(nb, me, ids):
    slot = lax.rem(nb, ELEM)
    away = jnp.where(nb // ELEM != me, 1.0, 0.0)
    stacked = jnp.concatenate([away, slot.astype(f32), jnp.zeros((116, LANES), f32)], axis=0).T
    row = iota2((ELEM, ELEM), 0)
    lane = iota2((ELEM, ELEM), 1)
    for face in range(4):
        rim = RIMS[face]
        away_col = stacked[:, face : face + 1]
        slot_col = stacked[:, 6 + face : 7 + face]
        away_row = away[face : face + 1]
        slot_row = slot[face : face + 1].astype(f32)
        upto = jnp.where(lane < row, jnp.broadcast_to(away_row, (ELEM, ELEM)), 0.0)
        rank_col = jnp.sum(upto, axis=1, keepdims=True)
        chosen = (away_col > 0.5) & (rank_col == lax.rem(lane, rim).astype(f32))
        order = jnp.sum(jnp.where(chosen, row.astype(f32), 0.0), axis=0, keepdims=True)
        ids[face] = jnp.broadcast_to(order.astype(jnp.int32), (NODES, LANES))
        mark = (away_col > 0.5) & (slot_col < slot_row)
        arrival = jnp.sum(jnp.where(mark, 1.0, 0.0), axis=0, keepdims=True)
        ids[4 + face] = jnp.broadcast_to(arrival.astype(jnp.int32), (NODES, LANES))
        ids[8 + face] = jnp.broadcast_to((away_row > 0.5).astype(jnp.int32), (NODES, LANES))
    for face in range(6):
        ids[12 + face] = jnp.broadcast_to(slot[face : face + 1], (NODES, LANES))


def project(src, fil, rot, finish):
    coef = [fil[n] for n in range(32)]

    def along_i(n, carry):
        f = n // NODES
        j = lax.rem(n, NODES)
        lines = filter_lines([src[f, i, j] for i in range(NODES)], coef)
        for i in range(NODES):
            src[f, i, j] = lines[i]
        return carry

    lax.fori_loop(0, FIELDS * NODES, along_i, 0, unroll=UNROLL)
    turn = [rot[r] for r in range(NODES)]

    def along_jl(n, carry):
        f = n // NODES
        i = lax.rem(n, NODES)
        lines = filter_lines([src[f, i, j] for j in range(NODES)], coef)
        for j in range(NODES):
            finish(f, i, j, rotated(lines[j], turn))
        return carry

    lax.fori_loop(0, FIELDS * NODES, along_jl, 0, unroll=UNROLL)


def volume_x(src, tend):
    def along_x(j, carry):
        fluxes = []
        for i in range(NODES):
            u = [src[f, i, j] for f in range(FIELDS)]
            fluxes.append(flux_of(u, primitive(u), 0))
        for f in range(FIELDS):
            lines = derive_lines([fluxes[i][f] for i in range(NODES)])
            for i in range(NODES):
                tend[f, i, j] = -lines[i]
        return carry

    lax.fori_loop(0, NODES, along_x, 0)


def volume_yz(src, tend, tab_ref):
    turn = [tab_ref[NCLS * NODES + r] for r in range(NODES)]

    def along_yz(i, carry):
        fluxes = []
        for j in range(NODES):
            u = [src[f, i, j] for f in range(FIELDS)]
            prim = primitive(u)
            fluxes.append(flux_of(u, prim, 1))
            along = flux_of(u, prim, 2)
            for f in range(FIELDS):
                tend[f, i, j] = tend[f, i, j] - rotated(along[f], turn)
        for f in range(FIELDS):
            lines = derive_lines([fluxes[j][f] for j in range(NODES)])
            for j in range(NODES):
                tend[f, i, j] = tend[f, i, j] - lines[j]
        return carry

    lax.fori_loop(0, NODES, along_yz, 0)


def jump(inner, outer, a, end):
    p_in = primitive(inner)
    p_out = primitive(outer)
    f_in = flux_of(inner, p_in, a)
    f_out = flux_of(outer, p_out, a)
    fastest = jnp.maximum(signal_of(p_in, a), signal_of(p_out, a))
    sign = -1.0 if end == 1 else 1.0
    out = []
    for f in range(FIELDS):
        out.append(sign * 0.5 * LIFT * (f_out[f] - f_in[f]) + 0.5 * LIFT * fastest * (outer[f] - inner[f]))
    return out


def faces_z(src, tend, ids):
    before, after = ids[16], ids[17]

    def z_faces(i, carry):
        low = [src.at[f, i].reshape(64, LANES)[pl.ds(0, 8, stride=8), :] for f in range(FIELDS)]
        high = [src.at[f, i].reshape(64, LANES)[pl.ds(7, 8, stride=8), :] for f in range(FIELDS)]
        add = jump(high, [take(low[f], after) for f in range(FIELDS)], 2, 1)
        for f in range(FIELDS):
            t = tend.at[f, i].reshape(64, LANES)
            t[pl.ds(7, 8, stride=8), :] = t[pl.ds(7, 8, stride=8), :] + add[f]
        add = jump(low, [take(high[f], before) for f in range(FIELDS)], 2, 0)
        for f in range(FIELDS):
            t = tend.at[f, i].reshape(64, LANES)
            t[pl.ds(0, 8, stride=8), :] = t[pl.ds(0, 8, stride=8), :] + add[f]
        return carry

    lax.fori_loop(0, NODES, z_faces, 0)


def face_tile(src, a, end, f, k):
    if a == 0:
        return src[f, 7 * end, k]
    return src[f, k, 7 * end]


def pack_faces(src, step, ids, packx, packy):
    lane8 = iota2((NODES, LANES), 1)
    for face in range(4):
        a, end = face // 2, face % 2
        order = ids[face]
        rim = RIMS[face]
        groups = LANES // rim
        width = 40 // groups
        pack = packx if a == 0 else packy
        for m in range(width):
            total = None
            for g in range(groups):
                t = g * width + m
                piece = take(face_tile(src, a, end, t // NODES, t % NODES), order)
                total = piece if total is None else jnp.where(lane8 >= g * rim, piece, total)
            pack[step, end, pl.ds(m * 8, 8), :] = total


def faces_xy(src, tend, step, ids, gotx, goty):
    for face in range(4):
        a, end = face // 2, face % 2
        rim = RIMS[face]
        width = 40 * rim // LANES
        got = gotx if a == 0 else goty
        local = ids[12 + face]
        arrival = ids[4 + face]
        remote = ids[8 + face] > 0
        for k in range(NODES):
            inner = [face_tile(src, a, end, f, k) for f in range(FIELDS)]
            outer = []
            for f in range(FIELDS):
                t = f * NODES + k
                near = take(face_tile(src, a, 1 - end, f, k), local)
                far = take(got[step, end, pl.ds((t % width) * 8, 8), :], arrival + (t // width) * rim)
                outer.append(jnp.where(remote, far, near))
            add = jump(inner, outer, a, end)
            for f in range(FIELDS):
                if a == 0:
                    tend[f, 7 * end, k] = tend[f, 7 * end, k] + add[f]
                else:
                    tend[f, k, 7 * end] = tend[f, k, 7 * end] + add[f]


def destinations(owner_row):
    owner = jnp.broadcast_to(owner_row, (ELEM, ELEM))
    owner_f = owner.astype(f32)
    same = owner_f == owner_f.T
    row = iota2((ELEM, ELEM), 0)
    rank = jnp.sum(jnp.where(same & (row < iota2((ELEM, ELEM), 1)), 1.0, 0.0), axis=0, keepdims=True)
    hit = row == owner
    first = jnp.where(hit & (rank < 0.5), 1.0, 0.0)
    second = jnp.where(hit & (rank > 0.5), 1.0, 0.0)
    return hit, first, second


def lanes_in(x, u):
    for f in range(FIELDS):
        for q in range(4):
            block = x[f, :, pl.ds(q * LANES, LANES)].T
            for p in range(16):
                u[f, q * 2 + p // 8, p % 8] = block[p * 8 : p * 8 + 8]


def lanes_out(u, out):
    def turn_back(n, carry):
        f = n // 4
        q = lax.rem(n, 4)
        block = u[f, pl.ds(q * 2, 2)].reshape(LANES, LANES)
        out[f, :, pl.ds(pl.multiple_of(q * LANES, LANES), LANES)] = block.T
        return carry

    lax.fori_loop(0, FIELDS * 4, turn_back, 0, unroll=2)


def stage_rows(u, first, second, stage):
    pick = jnp.concatenate([first, second], axis=0).astype(bf16)
    pick = jnp.concatenate([pick, pick], axis=1)
    for f in range(FIELDS):
        high, low = split_two(u[f].reshape(NQ, LANES))
        rows = lax.dot_general(
            pick, jnp.concatenate([high, low], axis=1), (((1,), (1,)), ((), ())), preferred_element_type=f32
        )
        for c in range(2):
            for q in range(4):
                stage[pl.ds(c * 20 + f * 4 + q, ELEM, stride=STRIDE), :] = rows[
                    c * ELEM : (c + 1) * ELEM, q * LANES : (q + 1) * LANES
                ]


def collect(landed, first, second, u):
    place = jnp.concatenate([first.T, second.T], axis=1).astype(bf16)
    place = jnp.concatenate([place, place], axis=1)
    for f in range(FIELDS):
        for q in range(4):
            r = f * 4 + q
            both = jnp.concatenate(
                [landed[pl.ds(r, ELEM, stride=STRIDE), :], landed[pl.ds(20 + r, ELEM, stride=STRIDE), :]], axis=0
            )
            high, low = split_two(both)
            block = jnp.dot(place, jnp.concatenate([high, low], axis=0), preferred_element_type=f32).T
            for p in range(16):
                u[f, q * 2 + p // 8, p % 8] = block[p * 8 : p * 8 + 8]


def kernel(
    x_hbm, owner_hbm, class_hbm, nb_hbm, tab_hbm, out_ref,
    x, owner, klass, nb, tab, stage, landed, u0, u1, tend, fil, rot, ids, packx, packy, gotx, goty,
    in_sem, send_sem, recv_sem, own_sem, ready, sx, rx, sy, ry,
):
    gx = lax.axis_index("gx")
    gy = lax.axis_index("gy")
    ngx = lax.axis_size("gx")
    ngy = lax.axis_size("gy")
    devices = ngx * ngy
    me = gx * ngy + gy
    barrier = pltpu.get_barrier_semaphore()

    loads = [
        pltpu.make_async_copy(a, b, in_sem.at[n])
        for n, (a, b) in enumerate(((owner_hbm, owner), (class_hbm, klass), (tab_hbm, tab), (x_hbm, x), (nb_hbm, nb)))
    ]
    for load in loads:
        load.start()

    def signal_row(sem):
        for r in range(1, ngy):
            pl.semaphore_signal(sem, inc=1, device_id=(gx, lax.rem(gy + r, ngy)), device_id_type=MESH)

    def signal_column(sem):
        for r in range(1, ngx):
            pl.semaphore_signal(sem, inc=1, device_id=(lax.rem(gx + r, ngx), gy), device_id_type=MESH)

    signal_row(barrier)
    signal_column(barrier)
    loads[0].wait()
    hit, first, second = destinations(owner[...])
    loads[1].wait()
    loads[2].wait()
    class_tables(klass[...].astype(f32), tab, fil, rot)
    pl.semaphore_wait(barrier, ngx + ngy - 2)
    signal_column(ready)

    loads[3].wait()
    lanes_in(x, u0)

    def put_initial(f, i, j, value):
        u0[f, i, j] = value

    project(u0, fil, rot, put_initial)
    stage_rows(u0, first, second, stage)
    stage[pl.ds(40, ELEM, stride=STRIDE), :] = jnp.broadcast_to(klass[...].astype(f32), (ELEM, ELEM))
    pl.semaphore_wait(ready, ngx - 1)

    def block(t):
        return pl.ds(pl.multiple_of(t * STRIDE, 8), ROWS)

    def exchange(t):
        return pltpu.make_async_remote_copy(
            src_ref=stage.at[block(t)],
            dst_ref=landed.at[block(me)],
            send_sem=send_sem,
            recv_sem=recv_sem,
            device_id=(t // ngy, lax.rem(t, ngy)),
            device_id_type=MESH,
        )

    own = pltpu.make_async_copy(stage.at[block(me)], landed.at[block(me)], own_sem)
    own.start()

    def send(r, carry):
        exchange(lax.rem(me + lax.rem(r * 37, devices), devices)).start()
        return carry

    lax.fori_loop(1, devices, send, 0)
    loads[4].wait()
    rim_tables(nb[...], me, ids)
    own.wait()

    total = pl.ds(0, (devices - 1) * ROWS)
    pltpu.make_async_copy(stage.at[total], landed.at[total], recv_sem).wait()
    collect(landed, first, second, u0)
    classes = landed[pl.ds(40, ELEM, stride=STRIDE), :]
    class_tables(jnp.sum(jnp.where(hit, classes, 0.0), axis=0, keepdims=True), tab, fil, rot)

    peers = [
        (lax.rem(gx + ngx - 1, ngx), gy),
        (lax.rem(gx + 1, ngx), gy),
        (gx, lax.rem(gy + ngy - 1, ngy)),
        (gx, lax.rem(gy + 1, ngy)),
    ]

    def rim_copies(step):
        out = []
        for face in range(4):
            pack, got, ss, rs = (packx, gotx, sx, rx) if face < 2 else (packy, goty, sy, ry)
            side = face % 2
            out.append(
                pltpu.make_async_remote_copy(
                    src_ref=pack.at[step, side],
                    dst_ref=got.at[step, 1 - side],
                    send_sem=ss.at[step, side],
                    recv_sem=rs.at[step, 1 - side],
                    device_id=peers[face],
                    device_id_type=MESH,
                )
            )
        return out

    def section(src, step, finish):
        pack_faces(src, step, ids, packx, packy)
        moving = rim_copies(step)
        for c in moving:
            c.start()
        volume_x(src, tend)
        volume_yz(src, tend, tab)
        faces_z(src, tend, ids)
        for c in moving:
            c.wait_recv()
        faces_xy(src, tend, step, ids, gotx, goty)
        project(tend, fil, rot, finish)
        return moving

    def put_first(f, i, j, value):
        u1[f, i, j] = u0[f, i, j] + time_step * value

    def put_last(f, i, j, value):
        u0[f, i, j] = 0.5 * u0[f, i, j] + 0.5 * (u1[f, i, j] + time_step * value)

    started = section(u0, 0, put_first)
    started = started + section(u1, 1, put_last)
    lanes_out(u0, out_ref)
    for c in started:
        c.wait_send()

    pltpu.make_async_copy(stage.at[total], landed.at[total], send_sem).wait()


def shards(conserved, order_class, new_owner, neighbours):
    dma = pltpu.SemaphoreType.DMA
    evolved = pl.pallas_call(
        kernel,
        out_shape=jax.ShapeDtypeStruct((FIELDS, ELEM, NQ), f32),
        in_specs=[pl.BlockSpec(memory_space=pltpu.HBM)] * 5,
        out_specs=pl.BlockSpec(memory_space=pltpu.VMEM),
        scratch_shapes=[
            pltpu.VMEM((FIELDS, ELEM, NQ), f32),
            pltpu.VMEM((1, ELEM), jnp.int32),
            pltpu.VMEM((1, ELEM), jnp.int32),
            pltpu.VMEM((6, ELEM), jnp.int32),
            pltpu.VMEM((48, NODES, LANES), f32),
            pltpu.VMEM((ELEM * STRIDE, LANES), f32),
            pltpu.VMEM((ELEM * STRIDE, LANES), f32),
            pltpu.VMEM(CUBE, f32),
            pltpu.VMEM(CUBE, f32),
            pltpu.VMEM(CUBE, f32),
            pltpu.VMEM((32, NODES, LANES), f32),
            pltpu.VMEM((NODES, NODES, LANES), f32),
            pltpu.VMEM((18, NODES, LANES), jnp.int32),
            pltpu.VMEM((2, 2, 80, LANES), f32),
            pltpu.VMEM((2, 2, 40, LANES), f32),
            pltpu.VMEM((2, 2, 80, LANES), f32),
            pltpu.VMEM((2, 2, 40, LANES), f32),
            dma((5,)),
            dma,
            dma,
            dma,
            pltpu.SemaphoreType.REGULAR,
            dma((2, 2)),
            dma((2, 2)),
            dma((2, 2)),
            dma((2, 2)),
        ],
        compiler_params=pltpu.CompilerParams(collective_id=0, has_side_effects=True, vmem_limit_bytes=61 << 20),
        name="flow",
    )(
        jnp.transpose(conserved, (1, 0, 2)),
        new_owner.reshape(1, ELEM),
        order_class.reshape(1, ELEM),
        jnp.transpose(neighbours, (1, 0)),
        jnp.asarray(rotation_tables()),
    )
    return jnp.transpose(evolved, (1, 0, 2))


def solution(mesh):
    in_specs = (
        P(("gx", "gy"), None, None),
        P(("gx", "gy")),
        P(("gx", "gy")),
        P(("gx", "gy"), None),
    )
    out_specs = P(("gx", "gy"), None, None)
    return jax.shard_map(shards, mesh=mesh, in_specs=in_specs, out_specs=out_specs, check_vma=False)
```

```python
import math

import jax
import jax.numpy as jnp
import numpy as np
from jax import lax
from jax.experimental import pallas as pl
from jax.experimental.pallas import tpu as pltpu
from jax.sharding import PartitionSpec as P

NODES = 8
NCLS = 5
FIELDS = 5
NQ = 512
ELEM = 128
LANES = 128
CUBE = (FIELDS, NODES, NODES, NODES, LANES)
heat_ratio = 1.4
rho_floor = 0.25
press_floor = 0.1
time_step = 0.005
MESH = pl.DeviceIdType.MESH
RIMS = (32, 32, 16, 16)
UNROLL = 4
BATCHES = ((0, 1), (1, 4), (4, 5))
f32 = jnp.float32
bf16 = jnp.bfloat16


def legendre_row(position, points):
    table = [1.0, position]
    for order in range(1, points - 1):
        table.append(
            ((2 * order + 1) * position * table[order] - order * table[order - 1]) / (order + 1)
        )
    return table[:points]


def node_tables(points, classes):
    degree = points - 1
    abscissae = [-math.cos(math.pi * index / degree) for index in range(points)]
    for newton_step in range(100):
        for index in range(1, degree):
            spot = abscissae[index]
            table = legendre_row(spot, points)
            abscissae[index] = spot - (spot * table[degree] - table[degree - 1]) / (
                points * table[degree]
            )
    vander = [legendre_row(spot, points) for spot in abscissae]
    values = [table[degree] for table in vander]
    weights = [2.0 / (degree * (degree + 1) * value * value) for value in values]
    derivative = np.zeros((points, points))
    for i in range(points):
        for j in range(points):
            if i != j:
                derivative[i, j] = values[i] / (values[j] * (abscissae[i] - abscissae[j]))
    derivative[0, 0] = -degree * (degree + 1) / 4.0
    derivative[degree, degree] = degree * (degree + 1) / 4.0
    vand = np.array(vander)
    wts = np.array(weights)
    norms = (wts[:, None] * vand**2).sum(axis=0)
    filters = np.zeros((classes, points, points))
    for k in range(classes):
        kept = degree - k + 1
        filters[k] = (vand[:, :kept] / norms[:kept]) @ (vand[:, :kept].T * wts)
    return derivative, filters, float(1.0 / weights[0])


DERIV, FILTERS, LIFT = node_tables(NODES, NCLS)
DER_ODD = 0.5 * (DERIV[:4, :4] - DERIV[:4, :3:-1])
DER_EVEN = 0.5 * (DERIV[:4, :4] + DERIV[:4, :3:-1])
FIL_EVEN = 0.5 * (FILTERS[:, :4, :4] + FILTERS[:, :4, :3:-1])
FIL_ODD = 0.5 * (FILTERS[:, :4, :4] - FILTERS[:, :4, :3:-1])


def rotation_tables():
    rows = np.arange(NODES)
    out = np.zeros((NODES * (NCLS + 1), NODES, LANES), np.float32)
    for r in range(NODES):
        for k in range(NCLS):
            out[k * NODES + r] = FILTERS[k][rows, (rows + r) % NODES][:, None]
        out[NCLS * NODES + r] = DERIV[rows, (rows + r) % NODES][:, None]
    return out


def split_two(value):
    high = value.astype(bf16)
    low = (value - high.astype(f32)).astype(bf16)
    return high, low


def iota2(shape, dim):
    return lax.broadcasted_iota(jnp.int32, shape, dim)


def mirrored(lines, even, odd):
    sums = [lines[m] + lines[7 - m] for m in range(4)]
    diffs = [lines[m] - lines[7 - m] for m in range(4)]
    top, bottom = [], []
    for k in range(4):
        a = even(k, 0) * sums[0]
        b = odd(k, 0) * diffs[0]
        for m in range(1, 4):
            a = a + even(k, m) * sums[m]
            b = b + odd(k, m) * diffs[m]
        top.append(a + b)
        bottom.append((a, b))
    return top, bottom


def filter_lines(lines, coef):
    top, parts = mirrored(lines, lambda k, m: coef[k * 4 + m], lambda k, m: coef[16 + k * 4 + m])
    return top + [parts[k][0] - parts[k][1] for k in (3, 2, 1, 0)]


def derive_lines(lines):
    top, parts = mirrored(lines, lambda k, m: float(DER_EVEN[k, m]), lambda k, m: float(DER_ODD[k, m]))
    return top + [parts[k][1] - parts[k][0] for k in (3, 2, 1, 0)]


def rotated(tile, coef):
    total = coef[0] * tile
    for r in range(1, NODES):
        total = total + coef[r] * pltpu.roll(tile, NODES - r, 0)
    return total


def primitive(u):
    inverse = 1.0 / jnp.maximum(u[0], rho_floor)
    vel = [u[1] * inverse, u[2] * inverse, u[3] * inverse]
    kinetic = 0.5 * (u[1] * vel[0] + u[2] * vel[1] + u[3] * vel[2])
    pressure = jnp.maximum((heat_ratio - 1.0) * (u[4] - kinetic), press_floor)
    return inverse, vel, pressure


def flux_of(u, prim, a):
    _, vel, pressure = prim
    v = vel[a]
    out = [u[1 + a]]
    for c in range(3):
        m = u[1 + c] * v
        out.append(m + pressure if c == a else m)
    out.append((u[4] + pressure) * v)
    return out


def signal_of(prim, a):
    inverse, vel, pressure = prim
    return jnp.abs(vel[a]) + jnp.sqrt(heat_ratio * pressure * inverse)


def take(tile, index):
    return jnp.take_along_axis(tile, index, axis=1)


def class_tables(cls, tab_ref, fil, rot):
    cls = jnp.broadcast_to(cls, (NODES, LANES))
    is_class = [jnp.where(cls == float(k), 1.0, 0.0) for k in range(NCLS)]
    for n in range(16):
        e = is_class[0] * float(FIL_EVEN[0, n // 4, n % 4])
        o = is_class[0] * float(FIL_ODD[0, n // 4, n % 4])
        for k in range(1, NCLS):
            e = e + is_class[k] * float(FIL_EVEN[k, n // 4, n % 4])
            o = o + is_class[k] * float(FIL_ODD[k, n // 4, n % 4])
        fil[n] = e
        fil[16 + n] = o
    for r in range(NODES):
        e = is_class[0] * tab_ref[r]
        for k in range(1, NCLS):
            e = e + is_class[k] * tab_ref[k * NODES + r]
        rot[r] = e


def rim_tables(nb, me, ids):
    slot = lax.rem(nb, ELEM)
    away = jnp.where(nb // ELEM != me, 1.0, 0.0)
    stacked = jnp.concatenate([away, slot.astype(f32), jnp.zeros((116, LANES), f32)], axis=0).T
    row = iota2((ELEM, ELEM), 0)
    lane = iota2((ELEM, ELEM), 1)
    for face in range(4):
        rim = RIMS[face]
        away_col = stacked[:, face : face + 1]
        slot_col = stacked[:, 6 + face : 7 + face]
        away_row = away[face : face + 1]
        slot_row = slot[face : face + 1].astype(f32)
        upto = jnp.where(lane < row, jnp.broadcast_to(away_row, (ELEM, ELEM)), 0.0)
        rank_col = jnp.sum(upto, axis=1, keepdims=True)
        chosen = (away_col > 0.5) & (rank_col == lax.rem(lane, rim).astype(f32))
        order = jnp.sum(jnp.where(chosen, row.astype(f32), 0.0), axis=0, keepdims=True)
        ids[face] = jnp.broadcast_to(order.astype(jnp.int32), (NODES, LANES))
        mark = (away_col > 0.5) & (slot_col < slot_row)
        arrival = jnp.sum(jnp.where(mark, 1.0, 0.0), axis=0, keepdims=True)
        ids[4 + face] = jnp.broadcast_to(arrival.astype(jnp.int32), (NODES, LANES))
        ids[8 + face] = jnp.broadcast_to((away_row > 0.5).astype(jnp.int32), (NODES, LANES))
    for face in range(6):
        ids[12 + face] = jnp.broadcast_to(slot[face : face + 1], (NODES, LANES))


def project(src, fil, rot, finish, fields=(0, FIELDS), after_field=None):
    coef = [fil[n] for n in range(32)]

    def along_i(n, carry):
        f = n // NODES
        j = lax.rem(n, NODES)
        lines = filter_lines([src[f, i, j] for i in range(NODES)], coef)
        for i in range(NODES):
            src[f, i, j] = lines[i]
        return carry

    lax.fori_loop(fields[0] * NODES, fields[1] * NODES, along_i, 0, unroll=UNROLL)
    turn = [rot[r] for r in range(NODES)]

    def along_jl(n, carry):
        f = n // NODES
        i = lax.rem(n, NODES)
        lines = filter_lines([src[f, i, j] for j in range(NODES)], coef)
        for j in range(NODES):
            finish(f, i, j, rotated(lines[j], turn))
        return carry

    if after_field is None:
        lax.fori_loop(fields[0] * NODES, fields[1] * NODES, along_jl, 0, unroll=UNROLL)
        return
    for f in range(FIELDS):
        lax.fori_loop(f * NODES, (f + 1) * NODES, along_jl, 0, unroll=UNROLL)
        after_field(f)


def volume_x(src, tend):
    def along_x(j, carry):
        fluxes = []
        for i in range(NODES):
            u = [src[f, i, j] for f in range(FIELDS)]
            fluxes.append(flux_of(u, primitive(u), 0))
        for f in range(FIELDS):
            lines = derive_lines([fluxes[i][f] for i in range(NODES)])
            for i in range(NODES):
                tend[f, i, j] = -lines[i]
        return carry

    lax.fori_loop(0, NODES, along_x, 0)


def volume_yz(src, tend, tab_ref):
    turn = [tab_ref[NCLS * NODES + r] for r in range(NODES)]

    def along_yz(i, carry):
        fluxes = []
        for j in range(NODES):
            u = [src[f, i, j] for f in range(FIELDS)]
            prim = primitive(u)
            fluxes.append(flux_of(u, prim, 1))
            along = flux_of(u, prim, 2)
            for f in range(FIELDS):
                tend[f, i, j] = tend[f, i, j] - rotated(along[f], turn)
        for f in range(FIELDS):
            lines = derive_lines([fluxes[j][f] for j in range(NODES)])
            for j in range(NODES):
                tend[f, i, j] = tend[f, i, j] - lines[j]
        return carry

    lax.fori_loop(0, NODES, along_yz, 0)


def jump(inner, outer, a, end):
    p_in = primitive(inner)
    p_out = primitive(outer)
    f_in = flux_of(inner, p_in, a)
    f_out = flux_of(outer, p_out, a)
    fastest = jnp.maximum(signal_of(p_in, a), signal_of(p_out, a))
    sign = -1.0 if end == 1 else 1.0
    out = []
    for f in range(FIELDS):
        out.append(sign * 0.5 * LIFT * (f_out[f] - f_in[f]) + 0.5 * LIFT * fastest * (outer[f] - inner[f]))
    return out


def faces_z(src, tend, ids):
    before, after = ids[16], ids[17]

    def z_faces(i, carry):
        low = [src.at[f, i].reshape(64, LANES)[pl.ds(0, 8, stride=8), :] for f in range(FIELDS)]
        high = [src.at[f, i].reshape(64, LANES)[pl.ds(7, 8, stride=8), :] for f in range(FIELDS)]
        add = jump(high, [take(low[f], after) for f in range(FIELDS)], 2, 1)
        for f in range(FIELDS):
            t = tend.at[f, i].reshape(64, LANES)
            t[pl.ds(7, 8, stride=8), :] = t[pl.ds(7, 8, stride=8), :] + add[f]
        add = jump(low, [take(high[f], before) for f in range(FIELDS)], 2, 0)
        for f in range(FIELDS):
            t = tend.at[f, i].reshape(64, LANES)
            t[pl.ds(0, 8, stride=8), :] = t[pl.ds(0, 8, stride=8), :] + add[f]
        return carry

    lax.fori_loop(0, NODES, z_faces, 0, unroll=True)


def face_tile(src, a, end, f, k):
    if a == 0:
        return src[f, 7 * end, k]
    return src[f, k, 7 * end]


def pack_faces(src, step, ids, packx, packy):
    lane8 = iota2((NODES, LANES), 1)
    for face in range(4):
        a, end = face // 2, face % 2
        order = ids[face]
        rim = RIMS[face]
        groups = LANES // rim
        width = 40 // groups
        pack = packx if a == 0 else packy
        for m in range(width):
            total = None
            for g in range(groups):
                t = g * width + m
                piece = take(face_tile(src, a, end, t // NODES, t % NODES), order)
                total = piece if total is None else jnp.where(lane8 >= g * rim, piece, total)
            pack[step, end, pl.ds(m * 8, 8), :] = total


def faces_xy(src, tend, step, ids, gotx, goty):
    for face in range(4):
        a, end = face // 2, face % 2
        rim = RIMS[face]
        width = 40 * rim // LANES
        got = gotx if a == 0 else goty
        local = ids[12 + face]
        arrival = ids[4 + face]
        remote = ids[8 + face] > 0
        for k in range(NODES):
            inner = [face_tile(src, a, end, f, k) for f in range(FIELDS)]
            outer = []
            for f in range(FIELDS):
                t = f * NODES + k
                near = take(face_tile(src, a, 1 - end, f, k), local)
                far = take(got[step, end, pl.ds((t % width) * 8, 8), :], arrival + (t // width) * rim)
                outer.append(jnp.where(remote, far, near))
            add = jump(inner, outer, a, end)
            for f in range(FIELDS):
                if a == 0:
                    tend[f, 7 * end, k] = tend[f, 7 * end, k] + add[f]
                else:
                    tend[f, k, 7 * end] = tend[f, k, 7 * end] + add[f]


def destinations(owner_row):
    owner = jnp.broadcast_to(owner_row, (ELEM, ELEM))
    owner_f = owner.astype(f32)
    same = owner_f == owner_f.T
    row = iota2((ELEM, ELEM), 0)
    rank = jnp.sum(jnp.where(same & (row < iota2((ELEM, ELEM), 1)), 1.0, 0.0), axis=0, keepdims=True)
    hit = row == owner
    first = jnp.where(hit & (rank < 0.5), 1.0, 0.0)
    second = jnp.where(hit & (rank > 0.5), 1.0, 0.0)
    return hit, first, second


def lanes_in(x, u, fields):
    for f in range(*fields):
        for q in range(4):
            block = x[f, :, pl.ds(q * LANES, LANES)].T
            for p in range(16):
                u[f, q * 2 + p // 8, p % 8] = block[p * 8 : p * 8 + 8]


def lanes_out_kernel(state_hbm, out_hbm, state, out, in_sem, out_sem):
    loads = [pltpu.make_async_copy(state_hbm.at[f], state.at[f], in_sem.at[f]) for f in range(FIELDS)]
    stores = [pltpu.make_async_copy(out.at[f], out_hbm.at[f], out_sem.at[f]) for f in range(FIELDS)]
    for load in loads:
        load.start()
    for f in range(FIELDS):
        loads[f].wait()
        for q in range(4):
            out[f, :, pl.ds(q * LANES, LANES)] = state[f, pl.ds(q * LANES, LANES), :].T
        stores[f].start()
    for store in stores:
        store.wait()


def lanes_out(state):
    return pl.pallas_call(
        lanes_out_kernel,
        out_shape=jax.ShapeDtypeStruct((FIELDS, ELEM, NQ), f32),
        in_specs=[pl.BlockSpec(memory_space=pltpu.HBM)],
        out_specs=pl.BlockSpec(memory_space=pltpu.HBM),
        scratch_shapes=[
            pltpu.VMEM((FIELDS, NQ, LANES), f32),
            pltpu.VMEM((FIELDS, ELEM, NQ), f32),
            pltpu.SemaphoreType.DMA((FIELDS,)),
            pltpu.SemaphoreType.DMA((FIELDS,)),
        ],
        compiler_params=pltpu.CompilerParams(vmem_limit_bytes=61 << 20),
        name="elements_first",
    )(state)


def batch_rows(fields):
    rows = (fields[1] - fields[0]) * 8
    if fields[0] == 0:
        return rows + 1, rows + 8
    return rows, rows


def stage_rows(u, pick, fields, stage):
    _, stride = batch_rows(fields)
    for f in range(*fields):
        high, low = split_two(u[f].reshape(NQ, LANES))
        rows = lax.dot_general(
            pick, jnp.concatenate([high, low], axis=1), (((1,), (1,)), ((), ())), preferred_element_type=f32
        )
        for c in range(2):
            for q in range(4):
                stage[pl.ds((f - fields[0]) * 8 + c * 4 + q, ELEM, stride=stride), :] = rows[
                    c * ELEM : (c + 1) * ELEM, q * LANES : (q + 1) * LANES
                ]


def collect(landed, place, fields, u):
    _, stride = batch_rows(fields)
    for f in range(*fields):
        parts = []
        for q in range(4):
            r = (f - fields[0]) * 8 + q
            parts.append(
                jnp.concatenate(
                    [landed[pl.ds(r, ELEM, stride=stride), :], landed[pl.ds(r + 4, ELEM, stride=stride), :]], axis=0
                )
            )
        high, low = split_two(jnp.concatenate(parts, axis=1))
        rows = jnp.dot(place, jnp.concatenate([high, low], axis=0), preferred_element_type=f32)
        for q in range(4):
            block = rows[:, q * LANES : (q + 1) * LANES].T
            for p in range(16):
                u[f, q * 2 + p // 8, p % 8] = block[p * 8 : p * 8 + 8]


def kernel(
    x_hbm, owner_hbm, class_hbm, nb_hbm, tab_hbm, out_ref,
    x, owner, klass, nb, tab, stages, landeds, u0, u1, tend, fil, rot, ids, packx, packy, gotx, goty,
    in_sem, out_sem, send_sem, recv_sem, own_sem, ready, sx, rx, sy, ry,
):
    gx = lax.axis_index("gx")
    gy = lax.axis_index("gy")
    ngx = lax.axis_size("gx")
    ngy = lax.axis_size("gy")
    devices = ngx * ngy
    me = gx * ngy + gy
    barrier = pltpu.get_barrier_semaphore()

    loads = [
        pltpu.make_async_copy(a, b, in_sem.at[n])
        for n, (a, b) in enumerate(
            ((owner_hbm, owner), (class_hbm, klass), (tab_hbm, tab), (nb_hbm, nb))
            + tuple((x_hbm.at[f], x.at[f]) for f in range(FIELDS))
        )
    ]
    for load in loads:
        load.start()

    def signal_row(sem):
        for r in range(1, ngy):
            pl.semaphore_signal(sem, inc=1, device_id=(gx, lax.rem(gy + r, ngy)), device_id_type=MESH)

    def signal_column(sem):
        for r in range(1, ngx):
            pl.semaphore_signal(sem, inc=1, device_id=(lax.rem(gx + r, ngx), gy), device_id_type=MESH)

    signal_row(barrier)
    signal_column(barrier)
    loads[0].wait()
    hit, first, second = destinations(owner[...])
    loads[1].wait()
    loads[2].wait()
    class_tables(klass[...].astype(f32), tab, fil, rot)
    pl.semaphore_wait(barrier, ngx + ngy - 2)
    signal_column(ready)

    pick = jnp.concatenate([first, second], axis=0).astype(bf16)
    pick = jnp.concatenate([pick, pick], axis=1)

    def put_initial(f, i, j, value):
        u0[f, i, j] = value

    def block(t, fields):
        rows, stride = batch_rows(fields)
        return pl.ds(pl.multiple_of(t * stride, 8), rows)

    def exchange(t, n):
        return pltpu.make_async_remote_copy(
            src_ref=stages[n].at[block(t, BATCHES[n])],
            dst_ref=landeds[n].at[block(me, BATCHES[n])],
            send_sem=send_sem.at[n],
            recv_sem=recv_sem.at[n],
            device_id=(t // ngy, lax.rem(t, ngy)),
            device_id_type=MESH,
        )

    owns = []
    for n, fields in enumerate(BATCHES):
        for f in range(*fields):
            loads[4 + f].wait()
        lanes_in(x, u0, fields)
        project(u0, fil, rot, put_initial, fields)
        stage_rows(u0, pick, fields, stages[n])
        if n == 0:
            rows, stride = batch_rows(fields)
            stages[n][pl.ds(rows - 1, ELEM, stride=stride), :] = jnp.broadcast_to(klass[...].astype(f32), (ELEM, ELEM))
            pl.semaphore_wait(ready, ngx - 1)
        here = block(me, fields)
        owns.append(pltpu.make_async_copy(stages[n].at[here], landeds[n].at[here], own_sem.at[n]))
        owns[n].start()

        def send(r, carry):
            exchange(lax.rem(me + lax.rem(r * 37, devices), devices), n).start()
            return carry

        lax.fori_loop(1, devices, send, 0)

    loads[3].wait()
    rim_tables(nb[...], me, ids)
    place = jnp.concatenate([first.T, second.T], axis=1).astype(bf16)
    place = jnp.concatenate([place, place], axis=1)
    for n, fields in enumerate(BATCHES):
        rows, stride = batch_rows(fields)
        whole = pl.ds(0, (devices - 1) * rows)
        owns[n].wait()
        pltpu.make_async_copy(stages[n].at[whole], landeds[n].at[whole], recv_sem.at[n]).wait()
        if n == 0:
            classes = landeds[n][pl.ds(rows - 1, ELEM, stride=stride), :]
            class_tables(jnp.sum(jnp.where(hit, classes, 0.0), axis=0, keepdims=True), tab, fil, rot)
        pltpu.make_async_copy(stages[n].at[whole], landeds[n].at[whole], send_sem.at[n]).wait()
        collect(landeds[n], place, fields, u0)

    peers = [
        (lax.rem(gx + ngx - 1, ngx), gy),
        (lax.rem(gx + 1, ngx), gy),
        (gx, lax.rem(gy + ngy - 1, ngy)),
        (gx, lax.rem(gy + 1, ngy)),
    ]

    def rim_copies(step):
        out = []
        for face in range(4):
            pack, got, ss, rs = (packx, gotx, sx, rx) if face < 2 else (packy, goty, sy, ry)
            side = face % 2
            out.append(
                pltpu.make_async_remote_copy(
                    src_ref=pack.at[step, side],
                    dst_ref=got.at[step, 1 - side],
                    send_sem=ss.at[step, side],
                    recv_sem=rs.at[step, 1 - side],
                    device_id=peers[face],
                    device_id_type=MESH,
                )
            )
        return out

    def section(src, step, finish, after_field=None):
        pack_faces(src, step, ids, packx, packy)
        moving = rim_copies(step)
        for c in moving:
            c.start()
        volume_x(src, tend)
        volume_yz(src, tend, tab)
        faces_z(src, tend, ids)
        for c in moving:
            c.wait_recv()
        faces_xy(src, tend, step, ids, gotx, goty)
        project(tend, fil, rot, finish, after_field=after_field)
        return moving

    def put_first(f, i, j, value):
        u1[f, i, j] = u0[f, i, j] + time_step * value

    def put_last(f, i, j, value):
        u0[f, i, j] = 0.5 * u0[f, i, j] + 0.5 * (u1[f, i, j] + time_step * value)

    started = section(u0, 0, put_first)
    results = [pltpu.make_async_copy(u0.at[f], out_ref.at[f], out_sem.at[f]) for f in range(FIELDS)]
    started = started + section(u1, 1, put_last, lambda f: results[f].start())
    for c in started:
        c.wait_send()

    for result in results:
        result.wait()


def shards(conserved, order_class, new_owner, neighbours):
    dma = pltpu.SemaphoreType.DMA
    evolved = pl.pallas_call(
        kernel,
        out_shape=jax.ShapeDtypeStruct(CUBE, f32),
        in_specs=[pl.BlockSpec(memory_space=pltpu.HBM)] * 5,
        out_specs=pl.BlockSpec(memory_space=pltpu.HBM),
        scratch_shapes=[
            pltpu.VMEM((FIELDS, ELEM, NQ), f32),
            pltpu.VMEM((1, ELEM), jnp.int32),
            pltpu.VMEM((1, ELEM), jnp.int32),
            pltpu.VMEM((6, ELEM), jnp.int32),
            pltpu.VMEM((48, NODES, LANES), f32),
            [pltpu.VMEM((ELEM * batch_rows(fields)[1], LANES), f32) for fields in BATCHES],
            [pltpu.VMEM((ELEM * batch_rows(fields)[1], LANES), f32) for fields in BATCHES],
            pltpu.VMEM(CUBE, f32),
            pltpu.VMEM(CUBE, f32),
            pltpu.VMEM(CUBE, f32),
            pltpu.VMEM((32, NODES, LANES), f32),
            pltpu.VMEM((NODES, NODES, LANES), f32),
            pltpu.VMEM((18, NODES, LANES), jnp.int32),
            pltpu.VMEM((2, 2, 80, LANES), f32),
            pltpu.VMEM((2, 2, 40, LANES), f32),
            pltpu.VMEM((2, 2, 80, LANES), f32),
            pltpu.VMEM((2, 2, 40, LANES), f32),
            dma((4 + FIELDS,)),
            dma((FIELDS,)),
            dma((len(BATCHES),)),
            dma((len(BATCHES),)),
            dma((len(BATCHES),)),
            pltpu.SemaphoreType.REGULAR,
            dma((2, 2)),
            dma((2, 2)),
            dma((2, 2)),
            dma((2, 2)),
        ],
        compiler_params=pltpu.CompilerParams(collective_id=0, has_side_effects=True, vmem_limit_bytes=61 << 20),
        name="flow",
    )(
        jnp.transpose(conserved, (1, 0, 2)),
        new_owner.reshape(1, ELEM),
        order_class.reshape(1, ELEM),
        jnp.transpose(neighbours, (1, 0)),
        jnp.asarray(rotation_tables()),
    )
    return jnp.transpose(lanes_out(evolved.reshape(FIELDS, NQ, LANES)), (1, 0, 2))


def solution(mesh):
    in_specs = (
        P(("gx", "gy"), None, None),
        P(("gx", "gy")),
        P(("gx", "gy")),
        P(("gx", "gy"), None),
    )
    out_specs = P(("gx", "gy"), None, None)
    return jax.shard_map(shards, mesh=mesh, in_specs=in_specs, out_specs=out_specs, check_vma=False)
```

```python
import math

import jax
import jax.numpy as jnp
import numpy as np
from jax import lax
from jax.experimental import pallas as pl
from jax.experimental.pallas import tpu as pltpu
from jax.sharding import PartitionSpec as P

NODES = 8
NCLS = 5
FIELDS = 5
NQ = 512
ELEM = 128
LANES = 128
CUBE = (FIELDS, NODES, NODES, NODES, LANES)
heat_ratio = 1.4
rho_floor = 0.25
press_floor = 0.1
time_step = 0.005
MESH = pl.DeviceIdType.MESH
RIMS = (32, 32, 16, 16)
UNROLL = 4
BATCHES = ((0, 1), (1, 4), (4, 5))
f32 = jnp.float32
bf16 = jnp.bfloat16


def legendre_row(position, points):
    table = [1.0, position]
    for order in range(1, points - 1):
        table.append(
            ((2 * order + 1) * position * table[order] - order * table[order - 1]) / (order + 1)
        )
    return table[:points]


def node_tables(points, classes):
    degree = points - 1
    abscissae = [-math.cos(math.pi * index / degree) for index in range(points)]
    for newton_step in range(100):
        for index in range(1, degree):
            spot = abscissae[index]
            table = legendre_row(spot, points)
            abscissae[index] = spot - (spot * table[degree] - table[degree - 1]) / (
                points * table[degree]
            )
    vander = [legendre_row(spot, points) for spot in abscissae]
    values = [table[degree] for table in vander]
    weights = [2.0 / (degree * (degree + 1) * value * value) for value in values]
    derivative = np.zeros((points, points))
    for i in range(points):
        for j in range(points):
            if i != j:
                derivative[i, j] = values[i] / (values[j] * (abscissae[i] - abscissae[j]))
    derivative[0, 0] = -degree * (degree + 1) / 4.0
    derivative[degree, degree] = degree * (degree + 1) / 4.0
    vand = np.array(vander)
    wts = np.array(weights)
    norms = (wts[:, None] * vand**2).sum(axis=0)
    filters = np.zeros((classes, points, points))
    for k in range(classes):
        kept = degree - k + 1
        filters[k] = (vand[:, :kept] / norms[:kept]) @ (vand[:, :kept].T * wts)
    return derivative, filters, float(1.0 / weights[0])


DERIV, FILTERS, LIFT = node_tables(NODES, NCLS)
DER_ODD = 0.5 * (DERIV[:4, :4] - DERIV[:4, :3:-1])
DER_EVEN = 0.5 * (DERIV[:4, :4] + DERIV[:4, :3:-1])
FIL_EVEN = 0.5 * (FILTERS[:, :4, :4] + FILTERS[:, :4, :3:-1])
FIL_ODD = 0.5 * (FILTERS[:, :4, :4] - FILTERS[:, :4, :3:-1])


def rotation_tables():
    rows = np.arange(NODES)
    out = np.zeros((NODES * (NCLS + 1), NODES, LANES), np.float32)
    for r in range(NODES):
        for k in range(NCLS):
            out[k * NODES + r] = FILTERS[k][rows, (rows + r) % NODES][:, None]
        out[NCLS * NODES + r] = DERIV[rows, (rows + r) % NODES][:, None]
    return out


def split_two(value):
    high = value.astype(bf16)
    low = (value - high.astype(f32)).astype(bf16)
    return high, low


def iota2(shape, dim):
    return lax.broadcasted_iota(jnp.int32, shape, dim)


def mirrored(lines, even, odd):
    sums = [lines[m] + lines[7 - m] for m in range(4)]
    diffs = [lines[m] - lines[7 - m] for m in range(4)]
    top, bottom = [], []
    for k in range(4):
        a = even(k, 0) * sums[0]
        b = odd(k, 0) * diffs[0]
        for m in range(1, 4):
            a = a + even(k, m) * sums[m]
            b = b + odd(k, m) * diffs[m]
        top.append(a + b)
        bottom.append((a, b))
    return top, bottom


def filter_lines(lines, coef):
    top, parts = mirrored(lines, lambda k, m: coef[k * 4 + m], lambda k, m: coef[16 + k * 4 + m])
    return top + [parts[k][0] - parts[k][1] for k in (3, 2, 1, 0)]


def derive_lines(lines):
    top, parts = mirrored(lines, lambda k, m: float(DER_EVEN[k, m]), lambda k, m: float(DER_ODD[k, m]))
    return top + [parts[k][1] - parts[k][0] for k in (3, 2, 1, 0)]


def rotated(tile, coef):
    total = coef[0] * tile
    for r in range(1, NODES):
        total = total + coef[r] * pltpu.roll(tile, NODES - r, 0)
    return total


def primitive(u):
    inverse = 1.0 / jnp.maximum(u[0], rho_floor)
    vel = [u[1] * inverse, u[2] * inverse, u[3] * inverse]
    kinetic = 0.5 * (u[1] * vel[0] + u[2] * vel[1] + u[3] * vel[2])
    pressure = jnp.maximum((heat_ratio - 1.0) * (u[4] - kinetic), press_floor)
    return inverse, vel, pressure


def recalled(u, inverse, pressure):
    return inverse, [u[1] * inverse, u[2] * inverse, u[3] * inverse], pressure


def flux_of(u, prim, a):
    _, vel, pressure = prim
    v = vel[a]
    out = [u[1 + a]]
    for c in range(3):
        m = u[1 + c] * v
        out.append(m + pressure if c == a else m)
    out.append((u[4] + pressure) * v)
    return out


def signal_of(prim, a):
    inverse, vel, pressure = prim
    return jnp.abs(vel[a]) + jnp.sqrt(heat_ratio * pressure * inverse)


def take(tile, index):
    return jnp.take_along_axis(tile, index, axis=1)


def class_tables(cls, tab_ref, fil, rot):
    cls = jnp.broadcast_to(cls, (NODES, LANES))
    is_class = [jnp.where(cls == float(k), 1.0, 0.0) for k in range(NCLS)]
    for n in range(16):
        e = is_class[0] * float(FIL_EVEN[0, n // 4, n % 4])
        o = is_class[0] * float(FIL_ODD[0, n // 4, n % 4])
        for k in range(1, NCLS):
            e = e + is_class[k] * float(FIL_EVEN[k, n // 4, n % 4])
            o = o + is_class[k] * float(FIL_ODD[k, n // 4, n % 4])
        fil[n] = e
        fil[16 + n] = o
    for r in range(NODES):
        e = is_class[0] * tab_ref[r]
        for k in range(1, NCLS):
            e = e + is_class[k] * tab_ref[k * NODES + r]
        rot[r] = e


def rim_tables(nb, me, ids):
    slot = lax.rem(nb, ELEM)
    away = jnp.where(nb // ELEM != me, 1.0, 0.0)
    stacked = jnp.concatenate([away, slot.astype(f32), jnp.zeros((116, LANES), f32)], axis=0).T
    row = iota2((ELEM, ELEM), 0)
    lane = iota2((ELEM, ELEM), 1)
    for face in range(4):
        rim = RIMS[face]
        away_col = stacked[:, face : face + 1]
        slot_col = stacked[:, 6 + face : 7 + face]
        away_row = away[face : face + 1]
        slot_row = slot[face : face + 1].astype(f32)
        upto = jnp.where(lane < row, jnp.broadcast_to(away_row, (ELEM, ELEM)), 0.0)
        rank_col = jnp.sum(upto, axis=1, keepdims=True)
        chosen = (away_col > 0.5) & (rank_col == lax.rem(lane, rim).astype(f32))
        order = jnp.sum(jnp.where(chosen, row.astype(f32), 0.0), axis=0, keepdims=True)
        ids[face] = jnp.broadcast_to(order.astype(jnp.int32), (NODES, LANES))
        mark = (away_col > 0.5) & (slot_col < slot_row)
        arrival = jnp.sum(jnp.where(mark, 1.0, 0.0), axis=0, keepdims=True)
        ids[4 + face] = jnp.broadcast_to(arrival.astype(jnp.int32), (NODES, LANES))
        ids[8 + face] = jnp.broadcast_to((away_row > 0.5).astype(jnp.int32), (NODES, LANES))
    for face in range(6):
        ids[12 + face] = jnp.broadcast_to(slot[face : face + 1], (NODES, LANES))


def project(src, fil, rot, finish, fields=(0, FIELDS), after_field=None):
    coef = [fil[n] for n in range(32)]

    def along_i(n, carry):
        f = n // NODES
        j = lax.rem(n, NODES)
        lines = filter_lines([src[f, i, j] for i in range(NODES)], coef)
        for i in range(NODES):
            src[f, i, j] = lines[i]
        return carry

    lax.fori_loop(fields[0] * NODES, fields[1] * NODES, along_i, 0, unroll=UNROLL)
    turn = [rot[r] for r in range(NODES)]

    def along_jl(n, carry):
        f = n // NODES
        i = lax.rem(n, NODES)
        lines = filter_lines([src[f, i, j] for j in range(NODES)], coef)
        for j in range(NODES):
            finish(f, i, j, rotated(lines[j], turn))
        return carry

    if after_field is None:
        lax.fori_loop(fields[0] * NODES, fields[1] * NODES, along_jl, 0, unroll=UNROLL)
        return
    for f in range(FIELDS):
        lax.fori_loop(f * NODES, (f + 1) * NODES, along_jl, 0, unroll=UNROLL)
        after_field(f)


def volume_x(src, tend, prims):
    def along_x(j, carry):
        fluxes = []
        for i in range(NODES):
            u = [src[f, i, j] for f in range(FIELDS)]
            prim = primitive(u)
            prims[0, i, j] = prim[0]
            prims[1, i, j] = prim[2]
            fluxes.append(flux_of(u, prim, 0))
        for f in range(FIELDS):
            lines = derive_lines([fluxes[i][f] for i in range(NODES)])
            for i in range(NODES):
                tend[f, i, j] = -lines[i]
        return carry

    lax.fori_loop(0, NODES, along_x, 0)


def volume_yz(src, tend, prims, tab_ref):
    turn = [tab_ref[NCLS * NODES + r] for r in range(NODES)]

    def along_yz(i, carry):
        fluxes = []
        for j in range(NODES):
            u = [src[f, i, j] for f in range(FIELDS)]
            prim = recalled(u, prims[0, i, j], prims[1, i, j])
            fluxes.append(flux_of(u, prim, 1))
            along = flux_of(u, prim, 2)
            for f in range(FIELDS):
                tend[f, i, j] = tend[f, i, j] - rotated(along[f], turn)
        for f in range(FIELDS):
            lines = derive_lines([fluxes[j][f] for j in range(NODES)])
            for j in range(NODES):
                tend[f, i, j] = tend[f, i, j] - lines[j]
        return carry

    lax.fori_loop(0, NODES, along_yz, 0)


def jump(inner, p_in, outer, a, end):
    p_out = primitive(outer)
    f_in = flux_of(inner, p_in, a)
    f_out = flux_of(outer, p_out, a)
    fastest = jnp.maximum(signal_of(p_in, a), signal_of(p_out, a))
    sign = -1.0 if end == 1 else 1.0
    out = []
    for f in range(FIELDS):
        out.append(sign * 0.5 * LIFT * (f_out[f] - f_in[f]) + 0.5 * LIFT * fastest * (outer[f] - inner[f]))
    return out


def faces_z(src, tend, prims, ids):
    before, after = ids[16], ids[17]

    def z_faces(i, carry):
        low = [src.at[f, i].reshape(64, LANES)[pl.ds(0, 8, stride=8), :] for f in range(FIELDS)]
        high = [src.at[f, i].reshape(64, LANES)[pl.ds(7, 8, stride=8), :] for f in range(FIELDS)]
        known = [
            [prims.at[n, i].reshape(64, LANES)[pl.ds(l, 8, stride=8), :] for n in range(2)] for l in (0, 7)
        ]
        add = jump(high, recalled(high, *known[1]), [take(low[f], after) for f in range(FIELDS)], 2, 1)
        for f in range(FIELDS):
            t = tend.at[f, i].reshape(64, LANES)
            t[pl.ds(7, 8, stride=8), :] = t[pl.ds(7, 8, stride=8), :] + add[f]
        add = jump(low, recalled(low, *known[0]), [take(high[f], before) for f in range(FIELDS)], 2, 0)
        for f in range(FIELDS):
            t = tend.at[f, i].reshape(64, LANES)
            t[pl.ds(0, 8, stride=8), :] = t[pl.ds(0, 8, stride=8), :] + add[f]
        return carry

    lax.fori_loop(0, NODES, z_faces, 0, unroll=True)


def face_tile(src, a, end, f, k):
    if a == 0:
        return src[f, 7 * end, k]
    return src[f, k, 7 * end]


def pack_faces(src, step, ids, packx, packy):
    lane8 = iota2((NODES, LANES), 1)
    for face in range(4):
        a, end = face // 2, face % 2
        order = ids[face]
        rim = RIMS[face]
        groups = LANES // rim
        width = 40 // groups
        pack = packx if a == 0 else packy
        for m in range(width):
            total = None
            for g in range(groups):
                t = g * width + m
                piece = take(face_tile(src, a, end, t // NODES, t % NODES), order)
                total = piece if total is None else jnp.where(lane8 >= g * rim, piece, total)
            pack[step, end, pl.ds(m * 8, 8), :] = total


def faces_xy(src, tend, prims, step, ids, gotx, goty):
    for face in range(4):
        a, end = face // 2, face % 2
        rim = RIMS[face]
        width = 40 * rim // LANES
        got = gotx if a == 0 else goty
        local = ids[12 + face]
        arrival = ids[4 + face]
        remote = ids[8 + face] > 0
        for k in range(NODES):
            inner = [face_tile(src, a, end, f, k) for f in range(FIELDS)]
            outer = []
            for f in range(FIELDS):
                t = f * NODES + k
                near = take(face_tile(src, a, 1 - end, f, k), local)
                far = take(got[step, end, pl.ds((t % width) * 8, 8), :], arrival + (t // width) * rim)
                outer.append(jnp.where(remote, far, near))
            known = [face_tile(prims, a, end, n, k) for n in range(2)]
            add = jump(inner, recalled(inner, *known), outer, a, end)
            for f in range(FIELDS):
                if a == 0:
                    tend[f, 7 * end, k] = tend[f, 7 * end, k] + add[f]
                else:
                    tend[f, k, 7 * end] = tend[f, k, 7 * end] + add[f]


def destinations(owner_row):
    owner = jnp.broadcast_to(owner_row, (ELEM, ELEM))
    owner_f = owner.astype(f32)
    same = owner_f == owner_f.T
    row = iota2((ELEM, ELEM), 0)
    rank = jnp.sum(jnp.where(same & (row < iota2((ELEM, ELEM), 1)), 1.0, 0.0), axis=0, keepdims=True)
    hit = row == owner
    first = jnp.where(hit & (rank < 0.5), 1.0, 0.0)
    second = jnp.where(hit & (rank > 0.5), 1.0, 0.0)
    return first, second, rank


def split_owner(owner_row, gys):
    column = owner_row // gys
    return column, owner_row - column * gys


def count_product(left, right, dims):
    return lax.dot_general(left.astype(bf16), right.astype(bf16), (dims, ((), ())), preferred_element_type=f32)


def class_rows_out(klass_row, owner_row, rank, gys):
    column, along = split_owner(owner_row, gys)
    left = jnp.where(iota2((ELEM, ELEM), 0) == 8 * column, jnp.broadcast_to(klass_row, (ELEM, ELEM)), 0.0)
    right = jnp.where(iota2((ELEM, ELEM), 0) == 2 * along + rank.astype(jnp.int32), 1.0, 0.0)
    return count_product(left, right, ((1,), (1,)))


def class_rows_turn(rows, gys):
    row = iota2((ELEM, ELEM), 0)
    lane = iota2((ELEM, ELEM), 1)
    used = lax.rem(row, 8) == 0
    rows = jnp.where(used, rows, 0.0)
    total = None
    for c in range(2):
        picks = jnp.where(used & (lane == row // 4 + c), 1.0, 0.0)
        piece = count_product(count_product(picks, rows, ((1,), (1,))), picks, ((1,), (0,)))
        total = piece if total is None else total + piece
    return total


def class_of_slots(rows, owner_row, rank, gys):
    column, along = split_owner(owner_row, gys)
    row = iota2((ELEM, ELEM), 0)
    rows = jnp.where((lax.rem(row, 8) == 0) & (row < 8 * gys), rows, 0.0)
    lanes = jnp.where(row == 2 * column + rank.astype(jnp.int32), 1.0, 0.0)
    found = count_product(rows, lanes, ((1,), (0,)))
    return jnp.sum(jnp.where(row == 8 * along, found, 0.0), axis=0, keepdims=True)


def lanes_in(x, u, fields):
    for f in range(*fields):
        for q in range(4):
            block = x[f, :, pl.ds(q * LANES, LANES)].T
            for p in range(16):
                u[f, q * 2 + p // 8, p % 8] = block[p * 8 : p * 8 + 8]


def lanes_out_kernel(state_hbm, out_hbm, state, out, in_sem, out_sem):
    loads = [pltpu.make_async_copy(state_hbm.at[f], state.at[f], in_sem.at[f]) for f in range(FIELDS)]
    stores = [pltpu.make_async_copy(out.at[f], out_hbm.at[f], out_sem.at[f]) for f in range(FIELDS)]
    for load in loads:
        load.start()
    for f in range(FIELDS):
        loads[f].wait()
        for q in range(4):
            out[f, :, pl.ds(q * LANES, LANES)] = state[f, pl.ds(q * LANES, LANES), :].T
        stores[f].start()
    for store in stores:
        store.wait()


def lanes_out(state):
    return pl.pallas_call(
        lanes_out_kernel,
        out_shape=jax.ShapeDtypeStruct((FIELDS, ELEM, NQ), f32),
        in_specs=[pl.BlockSpec(memory_space=pltpu.HBM)],
        out_specs=pl.BlockSpec(memory_space=pltpu.HBM),
        scratch_shapes=[
            pltpu.VMEM((FIELDS, NQ, LANES), f32),
            pltpu.VMEM((FIELDS, ELEM, NQ), f32),
            pltpu.SemaphoreType.DMA((FIELDS,)),
            pltpu.SemaphoreType.DMA((FIELDS,)),
        ],
        compiler_params=pltpu.CompilerParams(vmem_limit_bytes=61 << 20),
        name="elements_first",
    )(state)


def batch_rows(fields):
    rows = (fields[1] - fields[0]) * 8
    return rows, rows


def stage_rows(u, pick, fields, stage):
    _, stride = batch_rows(fields)
    for f in range(*fields):
        high, low = split_two(u[f].reshape(NQ, LANES))
        rows = lax.dot_general(
            pick, jnp.concatenate([high, low], axis=1), (((1,), (1,)), ((), ())), preferred_element_type=f32
        )
        for c in range(2):
            for q in range(4):
                stage[pl.ds((f - fields[0]) * 8 + c * 4 + q, ELEM, stride=stride), :] = rows[
                    c * ELEM : (c + 1) * ELEM, q * LANES : (q + 1) * LANES
                ]


def collect(landed, place, fields, u):
    _, stride = batch_rows(fields)
    for f in range(*fields):
        parts = []
        for q in range(4):
            r = (f - fields[0]) * 8 + q
            parts.append(
                jnp.concatenate(
                    [landed[pl.ds(r, ELEM, stride=stride), :], landed[pl.ds(r + 4, ELEM, stride=stride), :]], axis=0
                )
            )
        high, low = split_two(jnp.concatenate(parts, axis=1))
        rows = jnp.dot(place, jnp.concatenate([high, low], axis=0), preferred_element_type=f32)
        for q in range(4):
            block = rows[:, q * LANES : (q + 1) * LANES].T
            for p in range(16):
                u[f, q * 2 + p // 8, p % 8] = block[p * 8 : p * 8 + 8]


def kernel(
    x_hbm, owner_hbm, class_hbm, nb_hbm, tab_hbm, out_ref,
    x, owner, klass, nb, tab, stages, landeds, c1s, c1l, c2s, c2l, u0, u1, tend, prims, fil, rot, ids, packx, packy, gotx, goty,
    in_sem, out_sem, class_sem, send_sem, recv_sem, own_sem, ready, sx, rx, sy, ry,
):
    gx = lax.axis_index("gx")
    gy = lax.axis_index("gy")
    ngx = lax.axis_size("gx")
    ngy = lax.axis_size("gy")
    devices = ngx * ngy
    me = gx * ngy + gy
    barrier = pltpu.get_barrier_semaphore()

    loads = [
        pltpu.make_async_copy(a, b, in_sem.at[n])
        for n, (a, b) in enumerate(
            ((owner_hbm, owner), (class_hbm, klass), (tab_hbm, tab), (nb_hbm, nb))
            + tuple((x_hbm.at[f], x.at[f]) for f in range(FIELDS))
        )
    ]
    for load in loads:
        load.start()

    def signal_row(sem):
        for r in range(1, ngy):
            pl.semaphore_signal(sem, inc=1, device_id=(gx, lax.rem(gy + r, ngy)), device_id_type=MESH)

    def signal_column(sem):
        for r in range(1, ngx):
            pl.semaphore_signal(sem, inc=1, device_id=(lax.rem(gx + r, ngx), gy), device_id_type=MESH)

    signal_row(barrier)
    signal_column(barrier)
    loads[0].wait()
    first, second, rank = destinations(owner[...])
    loads[1].wait()
    loads[2].wait()
    class_tables(klass[...].astype(f32), tab, fil, rot)
    pl.semaphore_wait(barrier, ngx + ngy - 2)
    signal_column(ready)

    pick = jnp.concatenate([first, second], axis=0).astype(bf16)
    pick = jnp.concatenate([pick, pick], axis=1)

    def put_initial(f, i, j, value):
        u0[f, i, j] = value

    def block(t, fields):
        rows, stride = batch_rows(fields)
        return pl.ds(pl.multiple_of(t * stride, 8), rows)

    def exchange(t, n):
        return pltpu.make_async_remote_copy(
            src_ref=stages[n].at[block(t, BATCHES[n])],
            dst_ref=landeds[n].at[block(me, BATCHES[n])],
            send_sem=send_sem.at[n],
            recv_sem=recv_sem.at[n],
            device_id=(t // ngy, lax.rem(t, ngy)),
            device_id_type=MESH,
        )

    def hop(src, dst, t, mine, peer, sems):
        return pltpu.make_async_remote_copy(
            src_ref=src.at[pl.ds(pl.multiple_of(t * 8, 8), 1)],
            dst_ref=dst.at[pl.ds(pl.multiple_of(mine * 8, 8), 1)],
            send_sem=class_sem.at[sems],
            recv_sem=class_sem.at[sems + 1],
            device_id=peer,
            device_id_type=MESH,
        )

    def class_hop(src, dst, size, mine, peer_of, sems):
        here = pl.ds(pl.multiple_of(mine * 8, 8), 1)
        own = pltpu.make_async_copy(src.at[here], dst.at[here], class_sem.at[sems + 2])
        own.start()
        for r in range(1, size):
            t = lax.rem(mine + r, size)
            hop(src, dst, t, mine, peer_of(t), sems).start()
        return own

    def class_wait(src, dst, size, own, sems):
        every = pl.ds(0, size - 1)
        own.wait()
        pltpu.make_async_copy(src.at[every], dst.at[every], class_sem.at[sems]).wait()
        pltpu.make_async_copy(src.at[every], dst.at[every], class_sem.at[sems + 1]).wait()

    c1s[...] = class_rows_out(klass[...].astype(f32), owner[...], rank, ngy)
    owns = []
    for n, fields in enumerate(BATCHES):
        for f in range(*fields):
            loads[4 + f].wait()
        lanes_in(x, u0, fields)
        project(u0, fil, rot, put_initial, fields)
        stage_rows(u0, pick, fields, stages[n])
        if n == 0:
            pl.semaphore_wait(ready, ngx - 1)
            own_class = class_hop(c1s, c1l, ngx, gx, lambda t: (t, gy), 0)
        here = block(me, fields)
        owns.append(pltpu.make_async_copy(stages[n].at[here], landeds[n].at[here], own_sem.at[n]))
        owns[n].start()

        def send(r, carry):
            exchange(lax.rem(me + lax.rem(r * 37, devices), devices), n).start()
            return carry

        lax.fori_loop(1, devices, send, 0)

    loads[3].wait()
    rim_tables(nb[...], me, ids)
    class_wait(c1s, c1l, ngx, own_class, 0)
    c2s[...] = class_rows_turn(c1l[...], ngy)
    own_class = class_hop(c2s, c2l, ngy, gy, lambda t: (gx, t), 3)
    place = jnp.concatenate([first.T, second.T], axis=1).astype(bf16)
    place = jnp.concatenate([place, place], axis=1)
    class_wait(c2s, c2l, ngy, own_class, 3)
    class_tables(class_of_slots(c2l[...], owner[...], rank, ngy), tab, fil, rot)
    for n, fields in enumerate(BATCHES):
        rows, stride = batch_rows(fields)
        whole = pl.ds(0, (devices - 1) * rows)
        owns[n].wait()
        pltpu.make_async_copy(stages[n].at[whole], landeds[n].at[whole], recv_sem.at[n]).wait()
        pltpu.make_async_copy(stages[n].at[whole], landeds[n].at[whole], send_sem.at[n]).wait()
        collect(landeds[n], place, fields, u0)

    peers = [
        (lax.rem(gx + ngx - 1, ngx), gy),
        (lax.rem(gx + 1, ngx), gy),
        (gx, lax.rem(gy + ngy - 1, ngy)),
        (gx, lax.rem(gy + 1, ngy)),
    ]

    def rim_copies(step):
        out = []
        for face in range(4):
            pack, got, ss, rs = (packx, gotx, sx, rx) if face < 2 else (packy, goty, sy, ry)
            side = face % 2
            out.append(
                pltpu.make_async_remote_copy(
                    src_ref=pack.at[step, side],
                    dst_ref=got.at[step, 1 - side],
                    send_sem=ss.at[step, side],
                    recv_sem=rs.at[step, 1 - side],
                    device_id=peers[face],
                    device_id_type=MESH,
                )
            )
        return out

    def section(src, step, finish, after_field=None):
        pack_faces(src, step, ids, packx, packy)
        moving = rim_copies(step)
        for c in moving:
            c.start()
        volume_x(src, tend, prims)
        volume_yz(src, tend, prims, tab)
        faces_z(src, tend, prims, ids)
        for c in moving:
            c.wait_recv()
        faces_xy(src, tend, prims, step, ids, gotx, goty)
        project(tend, fil, rot, finish, after_field=after_field)
        return moving

    def put_first(f, i, j, value):
        u1[f, i, j] = u0[f, i, j] + time_step * value

    def put_last(f, i, j, value):
        u0[f, i, j] = 0.5 * u0[f, i, j] + 0.5 * (u1[f, i, j] + time_step * value)

    started = section(u0, 0, put_first)
    results = [pltpu.make_async_copy(u0.at[f], out_ref.at[f], out_sem.at[f]) for f in range(FIELDS)]
    started = started + section(u1, 1, put_last, lambda f: results[f].start())
    for c in started:
        c.wait_send()

    for result in results:
        result.wait()


def shards(conserved, order_class, new_owner, neighbours):
    dma = pltpu.SemaphoreType.DMA
    evolved = pl.pallas_call(
        kernel,
        out_shape=jax.ShapeDtypeStruct(CUBE, f32),
        in_specs=[pl.BlockSpec(memory_space=pltpu.HBM)] * 5,
        out_specs=pl.BlockSpec(memory_space=pltpu.HBM),
        scratch_shapes=[
            pltpu.VMEM((FIELDS, ELEM, NQ), f32),
            pltpu.VMEM((1, ELEM), jnp.int32),
            pltpu.VMEM((1, ELEM), jnp.int32),
            pltpu.VMEM((6, ELEM), jnp.int32),
            pltpu.VMEM((48, NODES, LANES), f32),
            [pltpu.VMEM((ELEM * batch_rows(fields)[1], LANES), f32) for fields in BATCHES],
            [pltpu.VMEM((ELEM * batch_rows(fields)[1], LANES), f32) for fields in BATCHES],
            pltpu.VMEM((ELEM, LANES), f32),
            pltpu.VMEM((ELEM, LANES), f32),
            pltpu.VMEM((ELEM, LANES), f32),
            pltpu.VMEM((ELEM, LANES), f32),
            pltpu.VMEM(CUBE, f32),
            pltpu.VMEM(CUBE, f32),
            pltpu.VMEM(CUBE, f32),
            pltpu.VMEM((2,) + CUBE[1:], f32),
            pltpu.VMEM((32, NODES, LANES), f32),
            pltpu.VMEM((NODES, NODES, LANES), f32),
            pltpu.VMEM((18, NODES, LANES), jnp.int32),
            pltpu.VMEM((2, 2, 80, LANES), f32),
            pltpu.VMEM((2, 2, 40, LANES), f32),
            pltpu.VMEM((2, 2, 80, LANES), f32),
            pltpu.VMEM((2, 2, 40, LANES), f32),
            dma((4 + FIELDS,)),
            dma((FIELDS,)),
            dma((6,)),
            dma((len(BATCHES),)),
            dma((len(BATCHES),)),
            dma((len(BATCHES),)),
            pltpu.SemaphoreType.REGULAR,
            dma((2, 2)),
            dma((2, 2)),
            dma((2, 2)),
            dma((2, 2)),
        ],
        compiler_params=pltpu.CompilerParams(collective_id=0, has_side_effects=True, vmem_limit_bytes=61 << 20),
        name="flow",
    )(
        jnp.transpose(conserved, (1, 0, 2)),
        new_owner.reshape(1, ELEM),
        order_class.reshape(1, ELEM),
        jnp.transpose(neighbours, (1, 0)),
        jnp.asarray(rotation_tables()),
    )
    return jnp.transpose(lanes_out(evolved.reshape(FIELDS, NQ, LANES)), (1, 0, 2))


def solution(mesh):
    in_specs = (
        P(("gx", "gy"), None, None),
        P(("gx", "gy")),
        P(("gx", "gy")),
        P(("gx", "gy"), None),
    )
    out_specs = P(("gx", "gy"), None, None)
    return jax.shard_map(shards, mesh=mesh, in_specs=in_specs, out_specs=out_specs, check_vma=False)
```

```python
import math

import jax
import jax.numpy as jnp
import numpy as np
from jax import lax
from jax.experimental import pallas as pl
from jax.experimental.pallas import tpu as pltpu
from jax.sharding import PartitionSpec as P

NODES = 8
NCLS = 5
FIELDS = 5
NQ = 512
ELEM = 128
LANES = 128
CUBE = (FIELDS, NODES, NODES, NODES, LANES)
heat_ratio = 1.4
rho_floor = 0.25
press_floor = 0.1
time_step = 0.005
MESH = pl.DeviceIdType.MESH
RIMS = (32, 32, 16, 16)
UNROLL = 4
BATCHES = ((0, 1), (1, 4), (4, 5))
f32 = jnp.float32
bf16 = jnp.bfloat16


def legendre_row(position, points):
    table = [1.0, position]
    for order in range(1, points - 1):
        table.append(
            ((2 * order + 1) * position * table[order] - order * table[order - 1]) / (order + 1)
        )
    return table[:points]


def node_tables(points, classes):
    degree = points - 1
    abscissae = [-math.cos(math.pi * index / degree) for index in range(points)]
    for newton_step in range(100):
        for index in range(1, degree):
            spot = abscissae[index]
            table = legendre_row(spot, points)
            abscissae[index] = spot - (spot * table[degree] - table[degree - 1]) / (
                points * table[degree]
            )
    vander = [legendre_row(spot, points) for spot in abscissae]
    values = [table[degree] for table in vander]
    weights = [2.0 / (degree * (degree + 1) * value * value) for value in values]
    derivative = np.zeros((points, points))
    for i in range(points):
        for j in range(points):
            if i != j:
                derivative[i, j] = values[i] / (values[j] * (abscissae[i] - abscissae[j]))
    derivative[0, 0] = -degree * (degree + 1) / 4.0
    derivative[degree, degree] = degree * (degree + 1) / 4.0
    vand = np.array(vander)
    wts = np.array(weights)
    norms = (wts[:, None] * vand**2).sum(axis=0)
    filters = np.zeros((classes, points, points))
    for k in range(classes):
        kept = degree - k + 1
        filters[k] = (vand[:, :kept] / norms[:kept]) @ (vand[:, :kept].T * wts)
    return derivative, filters, float(1.0 / weights[0])


DERIV, FILTERS, LIFT = node_tables(NODES, NCLS)
DER_ODD = 0.5 * (DERIV[:4, :4] - DERIV[:4, :3:-1])
DER_EVEN = 0.5 * (DERIV[:4, :4] + DERIV[:4, :3:-1])
FIL_EVEN = 0.5 * (FILTERS[:, :4, :4] + FILTERS[:, :4, :3:-1])
FIL_ODD = 0.5 * (FILTERS[:, :4, :4] - FILTERS[:, :4, :3:-1])


def rotation_tables():
    rows = np.arange(NODES)
    out = np.zeros((NODES * (NCLS + 1), NODES, LANES), np.float32)
    for r in range(NODES):
        for k in range(NCLS):
            out[k * NODES + r] = FILTERS[k][rows, (rows + r) % NODES][:, None]
        out[NCLS * NODES + r] = DERIV[rows, (rows + r) % NODES][:, None]
    return out


def split_two(value):
    high = value.astype(bf16)
    low = (value - high.astype(f32)).astype(bf16)
    return high, low


def iota2(shape, dim):
    return lax.broadcasted_iota(jnp.int32, shape, dim)


def mirrored(lines, even, odd):
    sums = [lines[m] + lines[7 - m] for m in range(4)]
    diffs = [lines[m] - lines[7 - m] for m in range(4)]
    top, bottom = [], []
    for k in range(4):
        a = even(k, 0) * sums[0]
        b = odd(k, 0) * diffs[0]
        for m in range(1, 4):
            a = a + even(k, m) * sums[m]
            b = b + odd(k, m) * diffs[m]
        top.append(a + b)
        bottom.append((a, b))
    return top, bottom


def filter_lines(lines, coef):
    top, parts = mirrored(lines, lambda k, m: coef[k * 4 + m], lambda k, m: coef[16 + k * 4 + m])
    return top + [parts[k][0] - parts[k][1] for k in (3, 2, 1, 0)]


def derive_lines(lines):
    top, parts = mirrored(lines, lambda k, m: float(DER_EVEN[k, m]), lambda k, m: float(DER_ODD[k, m]))
    return top + [parts[k][1] - parts[k][0] for k in (3, 2, 1, 0)]


def rotated(tile, coef):
    total = coef[0] * tile
    for r in range(1, NODES):
        total = total + coef[r] * pltpu.roll(tile, NODES - r, 0)
    return total


def primitive(u):
    inverse = 1.0 / jnp.maximum(u[0], rho_floor)
    vel = [u[1] * inverse, u[2] * inverse, u[3] * inverse]
    kinetic = 0.5 * (u[1] * vel[0] + u[2] * vel[1] + u[3] * vel[2])
    pressure = jnp.maximum((heat_ratio - 1.0) * (u[4] - kinetic), press_floor)
    return inverse, vel, pressure


def recalled(u, inverse, pressure):
    return inverse, [u[1] * inverse, u[2] * inverse, u[3] * inverse], pressure


def flux_of(u, prim, a):
    _, vel, pressure = prim
    v = vel[a]
    out = [u[1 + a]]
    for c in range(3):
        m = u[1 + c] * v
        out.append(m + pressure if c == a else m)
    out.append((u[4] + pressure) * v)
    return out


def signal_of(prim, a):
    inverse, vel, pressure = prim
    return jnp.abs(vel[a]) + jnp.sqrt(heat_ratio * pressure * inverse)


def take(tile, index):
    return jnp.take_along_axis(tile, index, axis=1)


def class_tables(cls, tab_ref, fil, rot):
    cls = jnp.broadcast_to(cls, (NODES, LANES))
    is_class = [jnp.where(cls == float(k), 1.0, 0.0) for k in range(NCLS)]
    for n in range(16):
        e = is_class[0] * float(FIL_EVEN[0, n // 4, n % 4])
        o = is_class[0] * float(FIL_ODD[0, n // 4, n % 4])
        for k in range(1, NCLS):
            e = e + is_class[k] * float(FIL_EVEN[k, n // 4, n % 4])
            o = o + is_class[k] * float(FIL_ODD[k, n // 4, n % 4])
        fil[n] = e
        fil[16 + n] = o
    for r in range(NODES):
        e = is_class[0] * tab_ref[r]
        for k in range(1, NCLS):
            e = e + is_class[k] * tab_ref[k * NODES + r]
        rot[r] = e


def rim_tables(nb, me, ids):
    slot = lax.rem(nb, ELEM)
    away = jnp.where(nb // ELEM != me, 1.0, 0.0)
    stacked = jnp.concatenate([away, slot.astype(f32), jnp.zeros((116, LANES), f32)], axis=0).T
    row = iota2((ELEM, ELEM), 0)
    lane = iota2((ELEM, ELEM), 1)
    for face in range(4):
        rim = RIMS[face]
        away_col = stacked[:, face : face + 1]
        slot_col = stacked[:, 6 + face : 7 + face]
        away_row = away[face : face + 1]
        slot_row = slot[face : face + 1].astype(f32)
        upto = jnp.where(lane < row, jnp.broadcast_to(away_row, (ELEM, ELEM)), 0.0)
        rank_col = jnp.sum(upto, axis=1, keepdims=True)
        chosen = (away_col > 0.5) & (rank_col == lax.rem(lane, rim).astype(f32))
        order = jnp.sum(jnp.where(chosen, row.astype(f32), 0.0), axis=0, keepdims=True)
        ids[face] = jnp.broadcast_to(order.astype(jnp.int32), (NODES, LANES))
        mark = (away_col > 0.5) & (slot_col < slot_row)
        arrival = jnp.sum(jnp.where(mark, 1.0, 0.0), axis=0, keepdims=True)
        ids[4 + face] = jnp.broadcast_to(arrival.astype(jnp.int32), (NODES, LANES))
        ids[8 + face] = jnp.broadcast_to((away_row > 0.5).astype(jnp.int32), (NODES, LANES))
    for face in range(6):
        ids[12 + face] = jnp.broadcast_to(slot[face : face + 1], (NODES, LANES))


def project(src, fil, rot, finish, fields=(0, FIELDS), after_field=None):
    coef = [fil[n] for n in range(32)]

    def along_i(n, carry):
        f = n // NODES
        j = lax.rem(n, NODES)
        lines = filter_lines([src[f, i, j] for i in range(NODES)], coef)
        for i in range(NODES):
            src[f, i, j] = lines[i]
        return carry

    lax.fori_loop(fields[0] * NODES, fields[1] * NODES, along_i, 0, unroll=UNROLL)
    turn = [rot[r] for r in range(NODES)]

    def along_jl(n, carry):
        f = n // NODES
        i = lax.rem(n, NODES)
        lines = filter_lines([src[f, i, j] for j in range(NODES)], coef)
        for j in range(NODES):
            finish(f, i, j, rotated(lines[j], turn))
        return carry

    if after_field is None:
        lax.fori_loop(fields[0] * NODES, fields[1] * NODES, along_jl, 0, unroll=UNROLL)
        return
    for f in range(FIELDS):
        lax.fori_loop(f * NODES, (f + 1) * NODES, along_jl, 0, unroll=UNROLL)
        after_field(f)


def volume_x(src, tend, prims):
    def along_x(j, carry):
        fluxes = []
        for i in range(NODES):
            u = [src[f, i, j] for f in range(FIELDS)]
            prim = primitive(u)
            prims[0, i, j] = prim[0]
            prims[1, i, j] = prim[2]
            fluxes.append(flux_of(u, prim, 0))
        for f in range(FIELDS):
            lines = derive_lines([fluxes[i][f] for i in range(NODES)])
            for i in range(NODES):
                tend[f, i, j] = -lines[i]
        return carry

    lax.fori_loop(0, NODES, along_x, 0)


def volume_yz(src, tend, prims, tab_ref):
    turn = [tab_ref[NCLS * NODES + r] for r in range(NODES)]

    def along_yz(i, carry):
        fluxes = []
        for j in range(NODES):
            u = [src[f, i, j] for f in range(FIELDS)]
            prim = recalled(u, prims[0, i, j], prims[1, i, j])
            fluxes.append(flux_of(u, prim, 1))
            along = flux_of(u, prim, 2)
            for f in range(FIELDS):
                tend[f, i, j] = tend[f, i, j] - rotated(along[f], turn)
        for f in range(FIELDS):
            lines = derive_lines([fluxes[j][f] for j in range(NODES)])
            for j in range(NODES):
                tend[f, i, j] = tend[f, i, j] - lines[j]
        return carry

    lax.fori_loop(0, NODES, along_yz, 0)


def jump(inner, p_in, outer, a, end):
    p_out = primitive(outer)
    f_in = flux_of(inner, p_in, a)
    f_out = flux_of(outer, p_out, a)
    fastest = jnp.maximum(signal_of(p_in, a), signal_of(p_out, a))
    sign = -1.0 if end == 1 else 1.0
    out = []
    for f in range(FIELDS):
        out.append(sign * 0.5 * LIFT * (f_out[f] - f_in[f]) + 0.5 * LIFT * fastest * (outer[f] - inner[f]))
    return out


def faces_z(src, tend, prims, ids):
    before, after = ids[16], ids[17]

    def z_faces(i, carry):
        low = [src.at[f, i].reshape(64, LANES)[pl.ds(0, 8, stride=8), :] for f in range(FIELDS)]
        high = [src.at[f, i].reshape(64, LANES)[pl.ds(7, 8, stride=8), :] for f in range(FIELDS)]
        known = [
            [prims.at[n, i].reshape(64, LANES)[pl.ds(l, 8, stride=8), :] for n in range(2)] for l in (0, 7)
        ]
        add = jump(high, recalled(high, *known[1]), [take(low[f], after) for f in range(FIELDS)], 2, 1)
        for f in range(FIELDS):
            t = tend.at[f, i].reshape(64, LANES)
            t[pl.ds(7, 8, stride=8), :] = t[pl.ds(7, 8, stride=8), :] + add[f]
        add = jump(low, recalled(low, *known[0]), [take(high[f], before) for f in range(FIELDS)], 2, 0)
        for f in range(FIELDS):
            t = tend.at[f, i].reshape(64, LANES)
            t[pl.ds(0, 8, stride=8), :] = t[pl.ds(0, 8, stride=8), :] + add[f]
        return carry

    lax.fori_loop(0, NODES, z_faces, 0, unroll=True)


def face_tile(src, a, end, f, k):
    if a == 0:
        return src[f, 7 * end, k]
    return src[f, k, 7 * end]


def pack_faces(src, step, ids, packx, packy):
    lane8 = iota2((NODES, LANES), 1)
    for face in range(4):
        a, end = face // 2, face % 2
        order = ids[face]
        rim = RIMS[face]
        groups = LANES // rim
        width = 40 // groups
        pack = packx if a == 0 else packy
        for m in range(width):
            total = None
            for g in range(groups):
                t = g * width + m
                piece = take(face_tile(src, a, end, t // NODES, t % NODES), order)
                total = piece if total is None else jnp.where(lane8 >= g * rim, piece, total)
            pack[step, end, pl.ds(m * 8, 8), :] = total


def near_traces(src, near, ids):
    for face in range(4):
        a, end = face // 2, face % 2
        local = ids[12 + face]
        for k in range(NODES):
            for f in range(FIELDS):
                near[face, f, k] = take(face_tile(src, a, 1 - end, f, k), local)


def faces_xy(src, tend, prims, near, step, ids, gotx, goty):
    for face in range(4):
        a, end = face // 2, face % 2
        rim = RIMS[face]
        width = 40 * rim // LANES
        got = gotx if a == 0 else goty
        arrival = ids[4 + face]
        remote = ids[8 + face] > 0
        for k in range(NODES):
            inner = [face_tile(src, a, end, f, k) for f in range(FIELDS)]
            outer = []
            for f in range(FIELDS):
                t = f * NODES + k
                far = take(got[step, end, pl.ds((t % width) * 8, 8), :], arrival + (t // width) * rim)
                outer.append(jnp.where(remote, far, near[face, f, k]))
            known = [face_tile(prims, a, end, n, k) for n in range(2)]
            add = jump(inner, recalled(inner, *known), outer, a, end)
            for f in range(FIELDS):
                if a == 0:
                    tend[f, 7 * end, k] = tend[f, 7 * end, k] + add[f]
                else:
                    tend[f, k, 7 * end] = tend[f, k, 7 * end] + add[f]


def destinations(owner_row):
    owner = jnp.broadcast_to(owner_row, (ELEM, ELEM))
    owner_f = owner.astype(f32)
    same = owner_f == owner_f.T
    row = iota2((ELEM, ELEM), 0)
    rank = jnp.sum(jnp.where(same & (row < iota2((ELEM, ELEM), 1)), 1.0, 0.0), axis=0, keepdims=True)
    hit = row == owner
    first = jnp.where(hit & (rank < 0.5), 1.0, 0.0)
    second = jnp.where(hit & (rank > 0.5), 1.0, 0.0)
    return first, second, rank


def split_owner(owner_row, gys):
    column = owner_row // gys
    return column, owner_row - column * gys


def count_product(left, right, dims):
    return lax.dot_general(left.astype(bf16), right.astype(bf16), (dims, ((), ())), preferred_element_type=f32)


def class_rows_out(klass_row, owner_row, rank, gys):
    column, along = split_owner(owner_row, gys)
    left = jnp.where(iota2((ELEM, ELEM), 0) == 8 * column, jnp.broadcast_to(klass_row, (ELEM, ELEM)), 0.0)
    right = jnp.where(iota2((ELEM, ELEM), 0) == 2 * along + rank.astype(jnp.int32), 1.0, 0.0)
    return count_product(left, right, ((1,), (1,)))


def class_rows_turn(rows, gys):
    row = iota2((ELEM, ELEM), 0)
    lane = iota2((ELEM, ELEM), 1)
    used = lax.rem(row, 8) == 0
    rows = jnp.where(used, rows, 0.0)
    total = None
    for c in range(2):
        picks = jnp.where(used & (lane == row // 4 + c), 1.0, 0.0)
        piece = count_product(count_product(picks, rows, ((1,), (1,))), picks, ((1,), (0,)))
        total = piece if total is None else total + piece
    return total


def class_of_slots(rows, owner_row, rank, gys):
    column, along = split_owner(owner_row, gys)
    row = iota2((ELEM, ELEM), 0)
    rows = jnp.where((lax.rem(row, 8) == 0) & (row < 8 * gys), rows, 0.0)
    lanes = jnp.where(row == 2 * column + rank.astype(jnp.int32), 1.0, 0.0)
    found = count_product(rows, lanes, ((1,), (0,)))
    return jnp.sum(jnp.where(row == 8 * along, found, 0.0), axis=0, keepdims=True)


def lanes_in(x, u, fields):
    for f in range(*fields):
        for q in range(4):
            block = x[f, :, pl.ds(q * LANES, LANES)].T
            for p in range(16):
                u[f, q * 2 + p // 8, p % 8] = block[p * 8 : p * 8 + 8]


def lanes_out_kernel(state_hbm, out_hbm, state, out, in_sem, out_sem):
    loads = [pltpu.make_async_copy(state_hbm.at[f], state.at[f], in_sem.at[f]) for f in range(FIELDS)]
    stores = [pltpu.make_async_copy(out.at[f], out_hbm.at[f], out_sem.at[f]) for f in range(FIELDS)]
    for load in loads:
        load.start()
    for f in range(FIELDS):
        loads[f].wait()
        for q in range(4):
            out[f, :, pl.ds(q * LANES, LANES)] = state[f, pl.ds(q * LANES, LANES), :].T
        stores[f].start()
    for store in stores:
        store.wait()


def lanes_out(state):
    return pl.pallas_call(
        lanes_out_kernel,
        out_shape=jax.ShapeDtypeStruct((FIELDS, ELEM, NQ), f32),
        in_specs=[pl.BlockSpec(memory_space=pltpu.HBM)],
        out_specs=pl.BlockSpec(memory_space=pltpu.HBM),
        scratch_shapes=[
            pltpu.VMEM((FIELDS, NQ, LANES), f32),
            pltpu.VMEM((FIELDS, ELEM, NQ), f32),
            pltpu.SemaphoreType.DMA((FIELDS,)),
            pltpu.SemaphoreType.DMA((FIELDS,)),
        ],
        compiler_params=pltpu.CompilerParams(vmem_limit_bytes=61 << 20),
        name="elements_first",
    )(state)


def batch_rows(fields):
    rows = (fields[1] - fields[0]) * 8
    return rows, rows


def stage_rows(u, pick, fields, stage):
    _, stride = batch_rows(fields)
    for f in range(*fields):
        high, low = split_two(u[f].reshape(NQ, LANES))
        rows = lax.dot_general(
            pick, jnp.concatenate([high, low], axis=1), (((1,), (1,)), ((), ())), preferred_element_type=f32
        )
        for c in range(2):
            for q in range(4):
                stage[pl.ds((f - fields[0]) * 8 + c * 4 + q, ELEM, stride=stride), :] = rows[
                    c * ELEM : (c + 1) * ELEM, q * LANES : (q + 1) * LANES
                ]


def collect(landed, place, fields, u):
    _, stride = batch_rows(fields)
    for f in range(*fields):
        parts = []
        for q in range(4):
            r = (f - fields[0]) * 8 + q
            parts.append(
                jnp.concatenate(
                    [landed[pl.ds(r, ELEM, stride=stride), :], landed[pl.ds(r + 4, ELEM, stride=stride), :]], axis=0
                )
            )
        high, low = split_two(jnp.concatenate(parts, axis=1))
        rows = jnp.dot(place, jnp.concatenate([high, low], axis=0), preferred_element_type=f32)
        for q in range(4):
            block = rows[:, q * LANES : (q + 1) * LANES].T
            for p in range(16):
                u[f, q * 2 + p // 8, p % 8] = block[p * 8 : p * 8 + 8]


def kernel(
    x_hbm, owner_hbm, class_hbm, nb_hbm, tab_hbm, out_ref,
    x, owner, klass, nb, tab, stages, landeds, c1s, c1l, c2s, c2l, u0, u1, tend, prims, near, fil, rot, ids, packx, packy, gotx, goty,
    in_sem, out_sem, class_sem, send_sem, recv_sem, own_sem, ready, sx, rx, sy, ry,
):
    gx = lax.axis_index("gx")
    gy = lax.axis_index("gy")
    ngx = lax.axis_size("gx")
    ngy = lax.axis_size("gy")
    devices = ngx * ngy
    me = gx * ngy + gy
    barrier = pltpu.get_barrier_semaphore()

    loads = [
        pltpu.make_async_copy(a, b, in_sem.at[n])
        for n, (a, b) in enumerate(
            ((owner_hbm, owner), (class_hbm, klass), (tab_hbm, tab), (nb_hbm, nb))
            + tuple((x_hbm.at[f], x.at[f]) for f in range(FIELDS))
        )
    ]
    for load in loads:
        load.start()

    def signal_row(sem):
        for r in range(1, ngy):
            pl.semaphore_signal(sem, inc=1, device_id=(gx, lax.rem(gy + r, ngy)), device_id_type=MESH)

    def signal_column(sem):
        for r in range(1, ngx):
            pl.semaphore_signal(sem, inc=1, device_id=(lax.rem(gx + r, ngx), gy), device_id_type=MESH)

    signal_row(barrier)
    signal_column(barrier)
    loads[0].wait()
    first, second, rank = destinations(owner[...])
    loads[1].wait()
    loads[2].wait()
    class_tables(klass[...].astype(f32), tab, fil, rot)
    pl.semaphore_wait(barrier, ngx + ngy - 2)
    signal_column(ready)

    pick = jnp.concatenate([first, second], axis=0).astype(bf16)
    pick = jnp.concatenate([pick, pick], axis=1)

    def put_initial(f, i, j, value):
        u0[f, i, j] = value

    def block(t, fields):
        rows, stride = batch_rows(fields)
        return pl.ds(pl.multiple_of(t * stride, 8), rows)

    def exchange(t, n):
        return pltpu.make_async_remote_copy(
            src_ref=stages[n].at[block(t, BATCHES[n])],
            dst_ref=landeds[n].at[block(me, BATCHES[n])],
            send_sem=send_sem.at[n],
            recv_sem=recv_sem.at[n],
            device_id=(t // ngy, lax.rem(t, ngy)),
            device_id_type=MESH,
        )

    def hop(src, dst, t, mine, peer, sems):
        return pltpu.make_async_remote_copy(
            src_ref=src.at[pl.ds(pl.multiple_of(t * 8, 8), 1)],
            dst_ref=dst.at[pl.ds(pl.multiple_of(mine * 8, 8), 1)],
            send_sem=class_sem.at[sems],
            recv_sem=class_sem.at[sems + 1],
            device_id=peer,
            device_id_type=MESH,
        )

    def class_hop(src, dst, size, mine, peer_of, sems):
        here = pl.ds(pl.multiple_of(mine * 8, 8), 1)
        own = pltpu.make_async_copy(src.at[here], dst.at[here], class_sem.at[sems + 2])
        own.start()
        for r in range(1, size):
            t = lax.rem(mine + r, size)
            hop(src, dst, t, mine, peer_of(t), sems).start()
        return own

    def class_wait(src, dst, size, own, sems):
        every = pl.ds(0, size - 1)
        own.wait()
        pltpu.make_async_copy(src.at[every], dst.at[every], class_sem.at[sems]).wait()
        pltpu.make_async_copy(src.at[every], dst.at[every], class_sem.at[sems + 1]).wait()

    c1s[...] = class_rows_out(klass[...].astype(f32), owner[...], rank, ngy)
    owns = []
    for n, fields in enumerate(BATCHES):
        for f in range(*fields):
            loads[4 + f].wait()
        lanes_in(x, u0, fields)
        project(u0, fil, rot, put_initial, fields)
        stage_rows(u0, pick, fields, stages[n])
        if n == 0:
            pl.semaphore_wait(ready, ngx - 1)
            own_class = class_hop(c1s, c1l, ngx, gx, lambda t: (t, gy), 0)
        here = block(me, fields)
        owns.append(pltpu.make_async_copy(stages[n].at[here], landeds[n].at[here], own_sem.at[n]))
        owns[n].start()

        def send(r, carry):
            exchange(lax.rem(me + lax.rem(r * 11, devices), devices), n).start()
            return carry

        lax.fori_loop(1, devices, send, 0)

    loads[3].wait()
    rim_tables(nb[...], me, ids)
    class_wait(c1s, c1l, ngx, own_class, 0)
    c2s[...] = class_rows_turn(c1l[...], ngy)
    own_class = class_hop(c2s, c2l, ngy, gy, lambda t: (gx, t), 3)
    place = jnp.concatenate([first.T, second.T], axis=1).astype(bf16)
    place = jnp.concatenate([place, place], axis=1)
    class_wait(c2s, c2l, ngy, own_class, 3)
    class_tables(class_of_slots(c2l[...], owner[...], rank, ngy), tab, fil, rot)
    for n, fields in enumerate(BATCHES):
        rows, stride = batch_rows(fields)
        whole = pl.ds(0, (devices - 1) * rows)
        owns[n].wait()
        pltpu.make_async_copy(stages[n].at[whole], landeds[n].at[whole], recv_sem.at[n]).wait()
        pltpu.make_async_copy(stages[n].at[whole], landeds[n].at[whole], send_sem.at[n]).wait()
        collect(landeds[n], place, fields, u0)

    peers = [
        (lax.rem(gx + ngx - 1, ngx), gy),
        (lax.rem(gx + 1, ngx), gy),
        (gx, lax.rem(gy + ngy - 1, ngy)),
        (gx, lax.rem(gy + 1, ngy)),
    ]

    def rim_copies(step):
        out = []
        for face in range(4):
            pack, got, ss, rs = (packx, gotx, sx, rx) if face < 2 else (packy, goty, sy, ry)
            side = face % 2
            out.append(
                pltpu.make_async_remote_copy(
                    src_ref=pack.at[step, side],
                    dst_ref=got.at[step, 1 - side],
                    send_sem=ss.at[step, side],
                    recv_sem=rs.at[step, 1 - side],
                    device_id=peers[face],
                    device_id_type=MESH,
                )
            )
        return out

    def section(src, step, finish, after_field=None):
        pack_faces(src, step, ids, packx, packy)
        moving = rim_copies(step)
        for c in moving:
            c.start()
        volume_x(src, tend, prims)
        volume_yz(src, tend, prims, tab)
        faces_z(src, tend, prims, ids)
        near_traces(src, near, ids)
        for c in moving:
            c.wait_recv()
        faces_xy(src, tend, prims, near, step, ids, gotx, goty)
        project(tend, fil, rot, finish, after_field=after_field)
        return moving

    def put_first(f, i, j, value):
        u1[f, i, j] = u0[f, i, j] + time_step * value

    def put_last(f, i, j, value):
        u0[f, i, j] = 0.5 * u0[f, i, j] + 0.5 * (u1[f, i, j] + time_step * value)

    started = section(u0, 0, put_first)
    results = [pltpu.make_async_copy(u0.at[f], out_ref.at[f], out_sem.at[f]) for f in range(FIELDS)]
    started = started + section(u1, 1, put_last, lambda f: results[f].start())
    for c in started:
        c.wait_send()

    for result in results:
        result.wait()


def shards(conserved, order_class, new_owner, neighbours):
    dma = pltpu.SemaphoreType.DMA
    evolved = pl.pallas_call(
        kernel,
        out_shape=jax.ShapeDtypeStruct(CUBE, f32),
        in_specs=[pl.BlockSpec(memory_space=pltpu.HBM)] * 5,
        out_specs=pl.BlockSpec(memory_space=pltpu.HBM),
        scratch_shapes=[
            pltpu.VMEM((FIELDS, ELEM, NQ), f32),
            pltpu.VMEM((1, ELEM), jnp.int32),
            pltpu.VMEM((1, ELEM), jnp.int32),
            pltpu.VMEM((6, ELEM), jnp.int32),
            pltpu.VMEM((48, NODES, LANES), f32),
            [pltpu.VMEM((ELEM * batch_rows(fields)[1], LANES), f32) for fields in BATCHES],
            [pltpu.VMEM((ELEM * batch_rows(fields)[1], LANES), f32) for fields in BATCHES],
            pltpu.VMEM((ELEM, LANES), f32),
            pltpu.VMEM((ELEM, LANES), f32),
            pltpu.VMEM((ELEM, LANES), f32),
            pltpu.VMEM((ELEM, LANES), f32),
            pltpu.VMEM(CUBE, f32),
            pltpu.VMEM(CUBE, f32),
            pltpu.VMEM(CUBE, f32),
            pltpu.VMEM((2,) + CUBE[1:], f32),
            pltpu.VMEM((4, FIELDS, NODES, NODES, LANES), f32),
            pltpu.VMEM((32, NODES, LANES), f32),
            pltpu.VMEM((NODES, NODES, LANES), f32),
            pltpu.VMEM((18, NODES, LANES), jnp.int32),
            pltpu.VMEM((2, 2, 80, LANES), f32),
            pltpu.VMEM((2, 2, 40, LANES), f32),
            pltpu.VMEM((2, 2, 80, LANES), f32),
            pltpu.VMEM((2, 2, 40, LANES), f32),
            dma((4 + FIELDS,)),
            dma((FIELDS,)),
            dma((6,)),
            dma((len(BATCHES),)),
            dma((len(BATCHES),)),
            dma((len(BATCHES),)),
            pltpu.SemaphoreType.REGULAR,
            dma((2, 2)),
            dma((2, 2)),
            dma((2, 2)),
            dma((2, 2)),
        ],
        compiler_params=pltpu.CompilerParams(collective_id=0, has_side_effects=True, vmem_limit_bytes=61 << 20),
        name="flow",
    )(
        jnp.transpose(conserved, (1, 0, 2)),
        new_owner.reshape(1, ELEM),
        order_class.reshape(1, ELEM),
        jnp.transpose(neighbours, (1, 0)),
        jnp.asarray(rotation_tables()),
    )
    return jnp.transpose(lanes_out(evolved.reshape(FIELDS, NQ, LANES)), (1, 0, 2))


def solution(mesh):
    in_specs = (
        P(("gx", "gy"), None, None),
        P(("gx", "gy")),
        P(("gx", "gy")),
        P(("gx", "gy"), None),
    )
    out_specs = P(("gx", "gy"), None, None)
    return jax.shard_map(shards, mesh=mesh, in_specs=in_specs, out_specs=out_specs, check_vma=False)
```

```python
import math

import jax
import jax.numpy as jnp
import numpy as np
from jax import lax
from jax.experimental import pallas as pl
from jax.experimental.pallas import tpu as pltpu
from jax.sharding import PartitionSpec as P

NODES = 8
NCLS = 5
FIELDS = 5
NQ = 512
ELEM = 128
LANES = 128
CUBE = (FIELDS, NODES, NODES, NODES, LANES)
heat_ratio = 1.4
rho_floor = 0.25
press_floor = 0.1
time_step = 0.005
MESH = pl.DeviceIdType.MESH
RIMS = (32, 32, 16, 16)
UNROLL = 4
BATCHES = ((0, 1), (1, 4), (4, 5))
f32 = jnp.float32
bf16 = jnp.bfloat16


def legendre_row(position, points):
    table = [1.0, position]
    for order in range(1, points - 1):
        table.append(
            ((2 * order + 1) * position * table[order] - order * table[order - 1]) / (order + 1)
        )
    return table[:points]


def node_tables(points, classes):
    degree = points - 1
    abscissae = [-math.cos(math.pi * index / degree) for index in range(points)]
    for newton_step in range(100):
        for index in range(1, degree):
            spot = abscissae[index]
            table = legendre_row(spot, points)
            abscissae[index] = spot - (spot * table[degree] - table[degree - 1]) / (
                points * table[degree]
            )
    vander = [legendre_row(spot, points) for spot in abscissae]
    values = [table[degree] for table in vander]
    weights = [2.0 / (degree * (degree + 1) * value * value) for value in values]
    derivative = np.zeros((points, points))
    for i in range(points):
        for j in range(points):
            if i != j:
                derivative[i, j] = values[i] / (values[j] * (abscissae[i] - abscissae[j]))
    derivative[0, 0] = -degree * (degree + 1) / 4.0
    derivative[degree, degree] = degree * (degree + 1) / 4.0
    vand = np.array(vander)
    wts = np.array(weights)
    norms = (wts[:, None] * vand**2).sum(axis=0)
    filters = np.zeros((classes, points, points))
    for k in range(classes):
        kept = degree - k + 1
        filters[k] = (vand[:, :kept] / norms[:kept]) @ (vand[:, :kept].T * wts)
    return derivative, filters, float(1.0 / weights[0])


DERIV, FILTERS, LIFT = node_tables(NODES, NCLS)
DER_ODD = 0.5 * (DERIV[:4, :4] - DERIV[:4, :3:-1])
DER_EVEN = 0.5 * (DERIV[:4, :4] + DERIV[:4, :3:-1])
FIL_EVEN = 0.5 * (FILTERS[:, :4, :4] + FILTERS[:, :4, :3:-1])
FIL_ODD = 0.5 * (FILTERS[:, :4, :4] - FILTERS[:, :4, :3:-1])


def rotation_tables():
    rows = np.arange(NODES)
    out = np.zeros((NODES * (NCLS + 1), NODES, LANES), np.float32)
    for r in range(NODES):
        for k in range(NCLS):
            out[k * NODES + r] = FILTERS[k][rows, (rows + r) % NODES][:, None]
        out[NCLS * NODES + r] = DERIV[rows, (rows + r) % NODES][:, None]
    return out


def split_two(value):
    high = value.astype(bf16)
    low = (value - high.astype(f32)).astype(bf16)
    return high, low


def iota2(shape, dim):
    return lax.broadcasted_iota(jnp.int32, shape, dim)


def mirrored(lines, even, odd):
    sums = [lines[m] + lines[7 - m] for m in range(4)]
    diffs = [lines[m] - lines[7 - m] for m in range(4)]
    top, bottom = [], []
    for k in range(4):
        a = even(k, 0) * sums[0]
        b = odd(k, 0) * diffs[0]
        for m in range(1, 4):
            a = a + even(k, m) * sums[m]
            b = b + odd(k, m) * diffs[m]
        top.append(a + b)
        bottom.append((a, b))
    return top, bottom


def filter_lines(lines, coef):
    top, parts = mirrored(lines, lambda k, m: coef[k * 4 + m], lambda k, m: coef[16 + k * 4 + m])
    return top + [parts[k][0] - parts[k][1] for k in (3, 2, 1, 0)]


def derive_lines(lines):
    top, parts = mirrored(lines, lambda k, m: float(DER_EVEN[k, m]), lambda k, m: float(DER_ODD[k, m]))
    return top + [parts[k][1] - parts[k][0] for k in (3, 2, 1, 0)]


def rotated(tile, coef):
    total = coef[0] * tile
    for r in range(1, NODES):
        total = total + coef[r] * pltpu.roll(tile, NODES - r, 0)
    return total


def primitive(u):
    inverse = 1.0 / jnp.maximum(u[0], rho_floor)
    vel = [u[1] * inverse, u[2] * inverse, u[3] * inverse]
    kinetic = 0.5 * (u[1] * vel[0] + u[2] * vel[1] + u[3] * vel[2])
    pressure = jnp.maximum((heat_ratio - 1.0) * (u[4] - kinetic), press_floor)
    return inverse, vel, pressure


def recalled(u, inverse, pressure):
    return inverse, [u[1] * inverse, u[2] * inverse, u[3] * inverse], pressure


def flux_of(u, prim, a):
    _, vel, pressure = prim
    v = vel[a]
    out = [u[1 + a]]
    for c in range(3):
        m = u[1 + c] * v
        out.append(m + pressure if c == a else m)
    out.append((u[4] + pressure) * v)
    return out


def signal_of(prim, a):
    inverse, vel, pressure = prim
    return jnp.abs(vel[a]) + jnp.sqrt(heat_ratio * pressure * inverse)


def take(tile, index):
    return jnp.take_along_axis(tile, index, axis=1)


def class_tables(cls, tab_ref, fil, rot):
    cls = jnp.broadcast_to(cls, (NODES, LANES))
    is_class = [jnp.where(cls == float(k), 1.0, 0.0) for k in range(NCLS)]
    for n in range(16):
        e = is_class[0] * float(FIL_EVEN[0, n // 4, n % 4])
        o = is_class[0] * float(FIL_ODD[0, n // 4, n % 4])
        for k in range(1, NCLS):
            e = e + is_class[k] * float(FIL_EVEN[k, n // 4, n % 4])
            o = o + is_class[k] * float(FIL_ODD[k, n // 4, n % 4])
        fil[n] = e
        fil[16 + n] = o
    for r in range(NODES):
        e = is_class[0] * tab_ref[r]
        for k in range(1, NCLS):
            e = e + is_class[k] * tab_ref[k * NODES + r]
        rot[r] = e


def rim_tables(nb, me, ids):
    slot = lax.rem(nb, ELEM)
    away = jnp.where(nb // ELEM != me, 1.0, 0.0)
    stacked = jnp.concatenate([away, slot.astype(f32), jnp.zeros((116, LANES), f32)], axis=0).T
    row = iota2((ELEM, ELEM), 0)
    lane = iota2((ELEM, ELEM), 1)
    for face in range(4):
        rim = RIMS[face]
        away_col = stacked[:, face : face + 1]
        slot_col = stacked[:, 6 + face : 7 + face]
        away_row = away[face : face + 1]
        slot_row = slot[face : face + 1].astype(f32)
        upto = jnp.where(lane < row, jnp.broadcast_to(away_row, (ELEM, ELEM)), 0.0)
        rank_col = jnp.sum(upto, axis=1, keepdims=True)
        chosen = (away_col > 0.5) & (rank_col == lax.rem(lane, rim).astype(f32))
        order = jnp.sum(jnp.where(chosen, row.astype(f32), 0.0), axis=0, keepdims=True)
        ids[face] = jnp.broadcast_to(order.astype(jnp.int32), (NODES, LANES))
        mark = (away_col > 0.5) & (slot_col < slot_row)
        arrival = jnp.sum(jnp.where(mark, 1.0, 0.0), axis=0, keepdims=True)
        ids[4 + face] = jnp.broadcast_to(arrival.astype(jnp.int32), (NODES, LANES))
        ids[8 + face] = jnp.broadcast_to((away_row > 0.5).astype(jnp.int32), (NODES, LANES))
    for face in range(6):
        ids[12 + face] = jnp.broadcast_to(slot[face : face + 1], (NODES, LANES))


def project(src, fil, rot, finish, fields=(0, FIELDS), after_field=None):
    coef = [fil[n] for n in range(32)]

    def along_i(n, carry):
        f = n // NODES
        j = lax.rem(n, NODES)
        lines = filter_lines([src[f, i, j] for i in range(NODES)], coef)
        for i in range(NODES):
            src[f, i, j] = lines[i]
        return carry

    lax.fori_loop(fields[0] * NODES, fields[1] * NODES, along_i, 0, unroll=UNROLL)
    turn = [rot[r] for r in range(NODES)]

    def along_jl(n, carry):
        f = n // NODES
        i = lax.rem(n, NODES)
        lines = filter_lines([src[f, i, j] for j in range(NODES)], coef)
        for j in range(NODES):
            finish(f, i, j, rotated(lines[j], turn))
        return carry

    if after_field is None:
        lax.fori_loop(fields[0] * NODES, fields[1] * NODES, along_jl, 0, unroll=UNROLL)
        return
    for f in range(FIELDS):
        lax.fori_loop(f * NODES, (f + 1) * NODES, along_jl, 0, unroll=UNROLL)
        after_field(f)


def volume_x(src, tend, prims):
    def along_x(j, carry):
        fluxes = []
        for i in range(NODES):
            u = [src[f, i, j] for f in range(FIELDS)]
            prim = primitive(u)
            prims[0, i, j] = prim[0]
            prims[1, i, j] = prim[2]
            fluxes.append(flux_of(u, prim, 0))
        for f in range(FIELDS):
            lines = derive_lines([fluxes[i][f] for i in range(NODES)])
            for i in range(NODES):
                tend[f, i, j] = -lines[i]
        return carry

    lax.fori_loop(0, NODES, along_x, 0)


def volume_yz(src, tend, prims, tab_ref):
    turn = [tab_ref[NCLS * NODES + r] for r in range(NODES)]

    def along_yz(i, carry):
        fluxes = []
        for j in range(NODES):
            u = [src[f, i, j] for f in range(FIELDS)]
            prim = recalled(u, prims[0, i, j], prims[1, i, j])
            fluxes.append(flux_of(u, prim, 1))
            along = flux_of(u, prim, 2)
            for f in range(FIELDS):
                tend[f, i, j] = tend[f, i, j] - rotated(along[f], turn)
        for f in range(FIELDS):
            lines = derive_lines([fluxes[j][f] for j in range(NODES)])
            for j in range(NODES):
                tend[f, i, j] = tend[f, i, j] - lines[j]
        return carry

    lax.fori_loop(0, NODES, along_yz, 0)


def jump(inner, p_in, outer, a, end):
    p_out = primitive(outer)
    f_in = flux_of(inner, p_in, a)
    f_out = flux_of(outer, p_out, a)
    fastest = jnp.maximum(signal_of(p_in, a), signal_of(p_out, a))
    sign = -1.0 if end == 1 else 1.0
    out = []
    for f in range(FIELDS):
        out.append(sign * 0.5 * LIFT * (f_out[f] - f_in[f]) + 0.5 * LIFT * fastest * (outer[f] - inner[f]))
    return out


def faces_z(src, tend, prims, ids):
    before, after = ids[16], ids[17]

    def z_faces(i, carry):
        low = [src.at[f, i].reshape(64, LANES)[pl.ds(0, 8, stride=8), :] for f in range(FIELDS)]
        high = [src.at[f, i].reshape(64, LANES)[pl.ds(7, 8, stride=8), :] for f in range(FIELDS)]
        known = [
            [prims.at[n, i].reshape(64, LANES)[pl.ds(l, 8, stride=8), :] for n in range(2)] for l in (0, 7)
        ]
        add = jump(high, recalled(high, *known[1]), [take(low[f], after) for f in range(FIELDS)], 2, 1)
        for f in range(FIELDS):
            t = tend.at[f, i].reshape(64, LANES)
            t[pl.ds(7, 8, stride=8), :] = t[pl.ds(7, 8, stride=8), :] + add[f]
        add = jump(low, recalled(low, *known[0]), [take(high[f], before) for f in range(FIELDS)], 2, 0)
        for f in range(FIELDS):
            t = tend.at[f, i].reshape(64, LANES)
            t[pl.ds(0, 8, stride=8), :] = t[pl.ds(0, 8, stride=8), :] + add[f]
        return carry

    lax.fori_loop(0, NODES, z_faces, 0, unroll=True)


def face_tile(src, a, end, f, k):
    if a == 0:
        return src[f, 7 * end, k]
    return src[f, k, 7 * end]


def pack_faces(src, step, ids, packx, packy):
    lane8 = iota2((NODES, LANES), 1)
    for face in range(4):
        a, end = face // 2, face % 2
        order = ids[face]
        rim = RIMS[face]
        groups = LANES // rim
        width = 40 // groups
        pack = packx if a == 0 else packy
        for m in range(width):
            total = None
            for g in range(groups):
                t = g * width + m
                piece = take(face_tile(src, a, end, t // NODES, t % NODES), order)
                total = piece if total is None else jnp.where(lane8 >= g * rim, piece, total)
            pack[step, end, pl.ds(m * 8, 8), :] = total


def near_traces(src, near, ids):
    for face in range(4):
        a, end = face // 2, face % 2
        local = ids[12 + face]
        for k in range(NODES):
            for f in range(FIELDS):
                near[face, f, k] = take(face_tile(src, a, 1 - end, f, k), local)


def faces_xy(src, tend, prims, near, step, ids, gotx, goty, faces):
    for face in faces:
        a, end = face // 2, face % 2
        rim = RIMS[face]
        width = 40 * rim // LANES
        got = gotx if a == 0 else goty
        arrival = ids[4 + face]
        remote = ids[8 + face] > 0
        for k in range(NODES):
            inner = [face_tile(src, a, end, f, k) for f in range(FIELDS)]
            outer = []
            for f in range(FIELDS):
                t = f * NODES + k
                far = take(got[step, end, pl.ds((t % width) * 8, 8), :], arrival + (t // width) * rim)
                outer.append(jnp.where(remote, far, near[face, f, k]))
            known = [face_tile(prims, a, end, n, k) for n in range(2)]
            add = jump(inner, recalled(inner, *known), outer, a, end)
            for f in range(FIELDS):
                if a == 0:
                    tend[f, 7 * end, k] = tend[f, 7 * end, k] + add[f]
                else:
                    tend[f, k, 7 * end] = tend[f, k, 7 * end] + add[f]


def destinations(owner_row):
    owner = jnp.broadcast_to(owner_row, (ELEM, ELEM))
    owner_f = owner.astype(f32)
    same = owner_f == owner_f.T
    row = iota2((ELEM, ELEM), 0)
    rank = jnp.sum(jnp.where(same & (row < iota2((ELEM, ELEM), 1)), 1.0, 0.0), axis=0, keepdims=True)
    hit = row == owner
    first = jnp.where(hit & (rank < 0.5), 1.0, 0.0)
    second = jnp.where(hit & (rank > 0.5), 1.0, 0.0)
    return first, second, rank


def split_owner(owner_row, gys):
    column = owner_row // gys
    return column, owner_row - column * gys


def count_product(left, right, dims):
    return lax.dot_general(left.astype(bf16), right.astype(bf16), (dims, ((), ())), preferred_element_type=f32)


def class_rows_out(klass_row, owner_row, rank, gys):
    column, along = split_owner(owner_row, gys)
    left = jnp.where(iota2((ELEM, ELEM), 0) == 8 * column, jnp.broadcast_to(klass_row, (ELEM, ELEM)), 0.0)
    right = jnp.where(iota2((ELEM, ELEM), 0) == 2 * along + rank.astype(jnp.int32), 1.0, 0.0)
    return count_product(left, right, ((1,), (1,)))


def class_rows_turn(rows, gys):
    row = iota2((ELEM, ELEM), 0)
    lane = iota2((ELEM, ELEM), 1)
    used = lax.rem(row, 8) == 0
    rows = jnp.where(used, rows, 0.0)
    total = None
    for c in range(2):
        picks = jnp.where(used & (lane == row // 4 + c), 1.0, 0.0)
        piece = count_product(count_product(picks, rows, ((1,), (1,))), picks, ((1,), (0,)))
        total = piece if total is None else total + piece
    return total


def class_of_slots(rows, owner_row, rank, gys):
    column, along = split_owner(owner_row, gys)
    row = iota2((ELEM, ELEM), 0)
    rows = jnp.where((lax.rem(row, 8) == 0) & (row < 8 * gys), rows, 0.0)
    lanes = jnp.where(row == 2 * column + rank.astype(jnp.int32), 1.0, 0.0)
    found = count_product(rows, lanes, ((1,), (0,)))
    return jnp.sum(jnp.where(row == 8 * along, found, 0.0), axis=0, keepdims=True)


def lanes_in(x, u, fields):
    for f in range(*fields):
        for q in range(4):
            block = x[f, :, pl.ds(q * LANES, LANES)].T
            for p in range(16):
                u[f, q * 2 + p // 8, p % 8] = block[p * 8 : p * 8 + 8]


def lanes_out_kernel(state_hbm, out_hbm, state, out, in_sem, out_sem):
    loads = [pltpu.make_async_copy(state_hbm.at[f], state.at[f], in_sem.at[f]) for f in range(FIELDS)]
    stores = [pltpu.make_async_copy(out.at[f], out_hbm.at[f], out_sem.at[f]) for f in range(FIELDS)]
    for load in loads:
        load.start()
    for f in range(FIELDS):
        loads[f].wait()
        for q in range(4):
            out[f, :, pl.ds(q * LANES, LANES)] = state[f, pl.ds(q * LANES, LANES), :].T
        stores[f].start()
    for store in stores:
        store.wait()


def lanes_out(state):
    return pl.pallas_call(
        lanes_out_kernel,
        out_shape=jax.ShapeDtypeStruct((FIELDS, ELEM, NQ), f32),
        in_specs=[pl.BlockSpec(memory_space=pltpu.HBM)],
        out_specs=pl.BlockSpec(memory_space=pltpu.HBM),
        scratch_shapes=[
            pltpu.VMEM((FIELDS, NQ, LANES), f32),
            pltpu.VMEM((FIELDS, ELEM, NQ), f32),
            pltpu.SemaphoreType.DMA((FIELDS,)),
            pltpu.SemaphoreType.DMA((FIELDS,)),
        ],
        compiler_params=pltpu.CompilerParams(vmem_limit_bytes=61 << 20),
        name="elements_first",
    )(state)


def batch_rows(fields):
    rows = (fields[1] - fields[0]) * 8
    return rows, rows


def stage_rows(u, pick, fields, stage):
    _, stride = batch_rows(fields)
    for f in range(*fields):
        high, low = split_two(u[f].reshape(NQ, LANES))
        rows = lax.dot_general(
            pick, jnp.concatenate([high, low], axis=1), (((1,), (1,)), ((), ())), preferred_element_type=f32
        )
        for c in range(2):
            for q in range(4):
                stage[pl.ds((f - fields[0]) * 8 + c * 4 + q, ELEM, stride=stride), :] = rows[
                    c * ELEM : (c + 1) * ELEM, q * LANES : (q + 1) * LANES
                ]


def collect(landed, place, fields, u):
    _, stride = batch_rows(fields)
    for f in range(*fields):
        parts = []
        for q in range(4):
            r = (f - fields[0]) * 8 + q
            parts.append(
                jnp.concatenate(
                    [landed[pl.ds(r, ELEM, stride=stride), :], landed[pl.ds(r + 4, ELEM, stride=stride), :]], axis=0
                )
            )
        high, low = split_two(jnp.concatenate(parts, axis=1))
        rows = jnp.dot(place, jnp.concatenate([high, low], axis=0), preferred_element_type=f32)
        for q in range(4):
            block = rows[:, q * LANES : (q + 1) * LANES].T
            for p in range(16):
                u[f, q * 2 + p // 8, p % 8] = block[p * 8 : p * 8 + 8]


def kernel(
    x_hbm, owner_hbm, class_hbm, nb_hbm, tab_hbm, out_ref,
    x, owner, klass, nb, tab, stages, landeds, c1s, c1l, c2s, c2l, u0, u1, tend, prims, near, fil, rot, ids, packx, packy, gotx, goty,
    in_sem, out_sem, class_sem, send_sem, recv_sem, own_sem, ready, sx, rx, sy, ry,
):
    gx = lax.axis_index("gx")
    gy = lax.axis_index("gy")
    ngx = lax.axis_size("gx")
    ngy = lax.axis_size("gy")
    devices = ngx * ngy
    me = gx * ngy + gy
    barrier = pltpu.get_barrier_semaphore()

    loads = [
        pltpu.make_async_copy(a, b, in_sem.at[n])
        for n, (a, b) in enumerate(
            ((owner_hbm, owner), (class_hbm, klass), (tab_hbm, tab), (nb_hbm, nb))
            + tuple((x_hbm.at[f], x.at[f]) for f in range(FIELDS))
        )
    ]
    for load in loads:
        load.start()

    def signal_row(sem):
        for r in range(1, ngy):
            pl.semaphore_signal(sem, inc=1, device_id=(gx, lax.rem(gy + r, ngy)), device_id_type=MESH)

    def signal_column(sem):
        for r in range(1, ngx):
            pl.semaphore_signal(sem, inc=1, device_id=(lax.rem(gx + r, ngx), gy), device_id_type=MESH)

    signal_row(barrier)
    signal_column(barrier)
    loads[0].wait()
    first, second, rank = destinations(owner[...])
    loads[1].wait()
    loads[2].wait()
    class_tables(klass[...].astype(f32), tab, fil, rot)
    pl.semaphore_wait(barrier, ngx + ngy - 2)
    signal_column(ready)

    pick = jnp.concatenate([first, second], axis=0).astype(bf16)
    pick = jnp.concatenate([pick, pick], axis=1)

    def put_initial(f, i, j, value):
        u0[f, i, j] = value

    def block(t, fields):
        rows, stride = batch_rows(fields)
        return pl.ds(pl.multiple_of(t * stride, 8), rows)

    def exchange(t, n):
        return pltpu.make_async_remote_copy(
            src_ref=stages[n].at[block(t, BATCHES[n])],
            dst_ref=landeds[n].at[block(me, BATCHES[n])],
            send_sem=send_sem.at[n],
            recv_sem=recv_sem.at[n],
            device_id=(t // ngy, lax.rem(t, ngy)),
            device_id_type=MESH,
        )

    def hop(src, dst, t, mine, peer, sems):
        return pltpu.make_async_remote_copy(
            src_ref=src.at[pl.ds(pl.multiple_of(t * 8, 8), 1)],
            dst_ref=dst.at[pl.ds(pl.multiple_of(mine * 8, 8), 1)],
            send_sem=class_sem.at[sems],
            recv_sem=class_sem.at[sems + 1],
            device_id=peer,
            device_id_type=MESH,
        )

    def class_hop(src, dst, size, mine, peer_of, sems):
        here = pl.ds(pl.multiple_of(mine * 8, 8), 1)
        own = pltpu.make_async_copy(src.at[here], dst.at[here], class_sem.at[sems + 2])
        own.start()
        for r in range(1, size):
            t = lax.rem(mine + r, size)
            hop(src, dst, t, mine, peer_of(t), sems).start()
        return own

    def class_wait(src, dst, size, own, sems):
        every = pl.ds(0, size - 1)
        own.wait()
        pltpu.make_async_copy(src.at[every], dst.at[every], class_sem.at[sems]).wait()
        pltpu.make_async_copy(src.at[every], dst.at[every], class_sem.at[sems + 1]).wait()

    c1s[...] = class_rows_out(klass[...].astype(f32), owner[...], rank, ngy)
    owns = []
    for n, fields in enumerate(BATCHES):
        for f in range(*fields):
            loads[4 + f].wait()
        lanes_in(x, u0, fields)
        project(u0, fil, rot, put_initial, fields)
        stage_rows(u0, pick, fields, stages[n])
        if n == 0:
            pl.semaphore_wait(ready, ngx - 1)
            own_class = class_hop(c1s, c1l, ngx, gx, lambda t: (t, gy), 0)
        here = block(me, fields)
        owns.append(pltpu.make_async_copy(stages[n].at[here], landeds[n].at[here], own_sem.at[n]))
        owns[n].start()

        def send(r, carry):
            exchange(lax.rem(me + lax.rem(r * 11, devices), devices), n).start()
            return carry

        lax.fori_loop(1, devices, send, 0)

    loads[3].wait()
    rim_tables(nb[...], me, ids)
    class_wait(c1s, c1l, ngx, own_class, 0)
    c2s[...] = class_rows_turn(c1l[...], ngy)
    own_class = class_hop(c2s, c2l, ngy, gy, lambda t: (gx, t), 3)
    place = jnp.concatenate([first.T, second.T], axis=1).astype(bf16)
    place = jnp.concatenate([place, place], axis=1)
    class_wait(c2s, c2l, ngy, own_class, 3)
    class_tables(class_of_slots(c2l[...], owner[...], rank, ngy), tab, fil, rot)
    for n, fields in enumerate(BATCHES):
        rows, stride = batch_rows(fields)
        whole = pl.ds(0, (devices - 1) * rows)
        owns[n].wait()
        pltpu.make_async_copy(stages[n].at[whole], landeds[n].at[whole], recv_sem.at[n]).wait()
        pltpu.make_async_copy(stages[n].at[whole], landeds[n].at[whole], send_sem.at[n]).wait()
        collect(landeds[n], place, fields, u0)

    peers = [
        (lax.rem(gx + ngx - 1, ngx), gy),
        (lax.rem(gx + 1, ngx), gy),
        (gx, lax.rem(gy + ngy - 1, ngy)),
        (gx, lax.rem(gy + 1, ngy)),
    ]

    def rim_copies(step):
        out = []
        for face in range(4):
            pack, got, ss, rs = (packx, gotx, sx, rx) if face < 2 else (packy, goty, sy, ry)
            side = face % 2
            out.append(
                pltpu.make_async_remote_copy(
                    src_ref=pack.at[step, side],
                    dst_ref=got.at[step, 1 - side],
                    send_sem=ss.at[step, side],
                    recv_sem=rs.at[step, 1 - side],
                    device_id=peers[face],
                    device_id_type=MESH,
                )
            )
        return out

    def section(src, step, finish, after_field=None):
        pack_faces(src, step, ids, packx, packy)
        moving = rim_copies(step)
        for c in moving:
            c.start()
        volume_x(src, tend, prims)
        volume_yz(src, tend, prims, tab)
        faces_z(src, tend, prims, ids)
        near_traces(src, near, ids)
        for faces in ((2, 3), (0, 1)):
            for face in faces:
                moving[face].wait_recv()
            faces_xy(src, tend, prims, near, step, ids, gotx, goty, faces)
        project(tend, fil, rot, finish, after_field=after_field)
        return moving

    def put_first(f, i, j, value):
        u1[f, i, j] = u0[f, i, j] + time_step * value

    def put_last(f, i, j, value):
        u0[f, i, j] = 0.5 * u0[f, i, j] + 0.5 * (u1[f, i, j] + time_step * value)

    started = section(u0, 0, put_first)
    results = [pltpu.make_async_copy(u0.at[f], out_ref.at[f], out_sem.at[f]) for f in range(FIELDS)]
    started = started + section(u1, 1, put_last, lambda f: results[f].start())
    for c in started:
        c.wait_send()

    for result in results:
        result.wait()


def shards(conserved, order_class, new_owner, neighbours):
    dma = pltpu.SemaphoreType.DMA
    evolved = pl.pallas_call(
        kernel,
        out_shape=jax.ShapeDtypeStruct(CUBE, f32),
        in_specs=[pl.BlockSpec(memory_space=pltpu.HBM)] * 5,
        out_specs=pl.BlockSpec(memory_space=pltpu.HBM),
        scratch_shapes=[
            pltpu.VMEM((FIELDS, ELEM, NQ), f32),
            pltpu.VMEM((1, ELEM), jnp.int32),
            pltpu.VMEM((1, ELEM), jnp.int32),
            pltpu.VMEM((6, ELEM), jnp.int32),
            pltpu.VMEM((48, NODES, LANES), f32),
            [pltpu.VMEM((ELEM * batch_rows(fields)[1], LANES), f32) for fields in BATCHES],
            [pltpu.VMEM((ELEM * batch_rows(fields)[1], LANES), f32) for fields in BATCHES],
            pltpu.VMEM((ELEM, LANES), f32),
            pltpu.VMEM((ELEM, LANES), f32),
            pltpu.VMEM((ELEM, LANES), f32),
            pltpu.VMEM((ELEM, LANES), f32),
            pltpu.VMEM(CUBE, f32),
            pltpu.VMEM(CUBE, f32),
            pltpu.VMEM(CUBE, f32),
            pltpu.VMEM((2,) + CUBE[1:], f32),
            pltpu.VMEM((4, FIELDS, NODES, NODES, LANES), f32),
            pltpu.VMEM((32, NODES, LANES), f32),
            pltpu.VMEM((NODES, NODES, LANES), f32),
            pltpu.VMEM((18, NODES, LANES), jnp.int32),
            pltpu.VMEM((2, 2, 80, LANES), f32),
            pltpu.VMEM((2, 2, 40, LANES), f32),
            pltpu.VMEM((2, 2, 80, LANES), f32),
            pltpu.VMEM((2, 2, 40, LANES), f32),
            dma((4 + FIELDS,)),
            dma((FIELDS,)),
            dma((6,)),
            dma((len(BATCHES),)),
            dma((len(BATCHES),)),
            dma((len(BATCHES),)),
            pltpu.SemaphoreType.REGULAR,
            dma((2, 2)),
            dma((2, 2)),
            dma((2, 2)),
            dma((2, 2)),
        ],
        compiler_params=pltpu.CompilerParams(collective_id=0, has_side_effects=True, vmem_limit_bytes=61 << 20),
        name="flow",
    )(
        jnp.transpose(conserved, (1, 0, 2)),
        new_owner.reshape(1, ELEM),
        order_class.reshape(1, ELEM),
        jnp.transpose(neighbours, (1, 0)),
        jnp.asarray(rotation_tables()),
    )
    return jnp.transpose(lanes_out(evolved.reshape(FIELDS, NQ, LANES)), (1, 0, 2))


def solution(mesh):
    in_specs = (
        P(("gx", "gy"), None, None),
        P(("gx", "gy")),
        P(("gx", "gy")),
        P(("gx", "gy"), None),
    )
    out_specs = P(("gx", "gy"), None, None)
    return jax.shard_map(shards, mesh=mesh, in_specs=in_specs, out_specs=out_specs, check_vma=False)
```
